128 devices in a mesh: oi: 8 (over y, z_hi), oj: 16 (over z_lo, x, core).
Axes of the slice: x: 4, y: 4, z: 4 (z_hi: 2, z_lo: 2; z = z_hi * 2 + z_lo), core: 2. Of those that a mesh axis runs over, the one named last changes fastest.
Arguments:
- b_tensor: bfloat16 [128, 1536, 512], P(('oi', 'oj')), may hold values from -2.5 to 2.5
- occ_energy: bfloat16 [128], P(('oi', 'oj')), may hold values from -2 to -0.29882812
- dom_blocks: int32 [128, 4], P(('oi', 'oj')), may hold values from 0 to 63
- pair_cols: int32 [128, 7], P(('oi', 'oj')), may hold values from 0 to 15, as said below
- pao_energy: float32 [64, 128], replicated, may hold values from 0.5 to 3
Outputs:
- gamma_tiles: bfloat16 [128, 1536, 512], P(('oi', 'oj'))
- aux_density: bfloat16 [1536, 1536], P(('oi', 'oj'))
The draws below stay inside these ranges and needn't reach their ends.
Inputs may be any that keep to these rules, and one draw needn't show every extreme that they name: `pair_cols`: each row names 7 different positions, never the orbital's own position o mod 16.
All inputs are finite; a program needn't handle non-finite values.
Results may differ from the reference program's by a relative error of at most 0.0031.
Values may be sent and summed in bfloat16 or wider, within the bound.
A program may use at most 128 MiB of HBM per device.

```python
import jax
import jax.numpy as jnp
from jax import lax

NAUX = 1536
PB = 128
DBLK = 4
NDOM = 512
NPB = 64
PAIRS = 7
NOCC = 128
N_OI = 8
N_OJ = 16


def draw_pair_cols(key, part):
    key = jax.random.fold_in(key, 11)
    first_key, second_key = jax.random.split(key)
    noise = jax.random.randint(first_key, (NOCC, N_OJ), 0, 256)
    popular = jax.random.randint(second_key, (N_OI, N_OJ), 0, 3)
    popular = popular.at[0, N_OJ - 1].set(3)
    orbitals = jnp.arange(NOCC)
    row_index = orbitals // N_OJ
    own_place = orbitals % N_OJ
    places = jnp.arange(N_OJ)
    scores = noise + 256 * popular[row_index]
    scores = jnp.where(places[None, :] == own_place[:, None], -1, scores)
    scores = scores * N_OJ + places[None, :]
    unused, chosen = lax.top_k(scores, PAIRS)
    return chosen.astype(jnp.int32)


def set_ends(result, key, smallest, high):
    spot = [jax.random.randint(jax.random.fold_in(key, axis), (), 0, length) for axis, length in enumerate(result.shape)]
    longest = result.shape.index(max(result.shape))
    beside = spot[:longest] + [(spot[longest] + 1) % result.shape[longest]] + spot[longest + 1:]
    return result.at[tuple(spot)].set(smallest).at[tuple(beside)].set(high)


def spiked(entries, key, source, target, shards_of, factor):
    def block_of(dim):
        return (jnp.arange(entries.shape[dim]) // (entries.shape[dim] // shards_of)).reshape((-1,) + (1,) * (entries.ndim - 1 - dim))

    one_side = jax.random.permutation(key, shards_of)[block_of(target)]
    second = (block_of(target) + shards_of // 2) % shards_of
    return jnp.where((block_of(source) == one_side) | (block_of(source) == second), factor * entries, entries)


def block_scale(own_key, shape, shards, smallest, high):
    level, own = 1.0, jax.random.fold_in(own_key, 6)
    for position, blocks in shards:
        heights = jnp.exp(jax.random.uniform(jax.random.fold_in(own, position), (blocks,), jnp.float32, smallest / len(shards), high / len(shards)))
        level = level * jnp.repeat(heights, shape[position] // blocks).reshape([-1 if axis == position else 1 for axis in range(len(shape))])
    return level


def noise_with(stream_key, dims, spread, most, cuts, heavy, kind=jnp.bfloat16):
    values = spread * jax.random.normal(stream_key, dims, jnp.float32)
    if cuts:
        values = values * block_scale(stream_key, dims, cuts, -0.22, 0.18)
    return jnp.clip(spiked(values, jax.random.fold_in(stream_key, 3), *heavy), -most, most).astype(kind)


def setup_inputs(seed: int = 0) -> dict:
    keys = jax.random.split(jax.random.key(seed), 6)
    b_tensor = noise_with(keys[0], (NOCC, NAUX, NDOM), 0.1, 2.5, ((0, 128),), (0, 1, 128, 5.5))
    occ_energy = jnp.clip(-2.0 + 1.7011719 * jax.random.uniform(keys[1], (NOCC,), jnp.float32) ** block_scale(keys[1], (NOCC,), ((0, 128),), -0.2, 0.2), -2.0, -0.29882812).astype(jnp.bfloat16)
    dom_blocks = set_ends(jax.random.randint(keys[2], (NOCC, DBLK), 0, NPB), jax.random.fold_in(keys[2], 1), 0, NPB - 1).astype(jnp.int32)
    pair_cols = draw_pair_cols(jax.random.fold_in(keys[5], 71), 0)
    pao_energy = jnp.clip(jax.random.uniform(keys[4], (NPB, PB), jnp.float32, 0.5, 3.0), 0.5, 3.0)
    return dict(b_tensor=b_tensor, occ_energy=occ_energy, dom_blocks=dom_blocks, pair_cols=pair_cols, pao_energy=pao_energy)


def reference(b_tensor, occ_energy, dom_blocks, pair_cols, pao_energy):
    virtual = pao_energy[dom_blocks].reshape(NOCC, NDOM).astype(jnp.float32)
    occupied = occ_energy.astype(jnp.float32)

    def visit(step_index, gamma_all):
        orbital = (step_index // PAIRS).astype(jnp.int32)
        pair_slot = (step_index % PAIRS).astype(jnp.int32)
        partner = ((orbital // N_OJ) * N_OJ + pair_cols[orbital, pair_slot]).astype(jnp.int32)
        orbital_block = b_tensor[orbital]
        partner_block = b_tensor[partner]
        intersection = lax.dot_general(orbital_block, partner_block, (((0,), (0,)), ((), ())), preferred_element_type=jnp.float32)
        denominator = virtual[orbital][:, None] + virtual[partner][None, :] - occupied[orbital] - occupied[partner]
        tile = (-intersection / denominator).astype(jnp.bfloat16)
        own_part = lax.dot_general(partner_block, tile, (((1,), (1,)), ((), ())), preferred_element_type=jnp.float32)
        mirror_part = jnp.dot(orbital_block, tile, preferred_element_type=jnp.float32)
        gamma_all = gamma_all.at[orbital].add(own_part)
        gamma_all = gamma_all.at[partner].add(mirror_part)
        return gamma_all

    gamma_all = lax.fori_loop(0, NOCC * PAIRS, visit, jnp.zeros((NOCC, NAUX, NDOM), jnp.float32))
    gamma_tiles = gamma_all.astype(jnp.bfloat16)
    factor = 1.0 / NOCC

    def collect(total_sum, items):
        gamma_one, block_one = items
        return total_sum + factor * lax.dot_general(gamma_one, block_one, (((1,), (1,)), ((), ())), preferred_element_type=jnp.float32), None

    density, unused = lax.scan(collect, jnp.zeros((NAUX, NAUX), jnp.float32), (gamma_tiles, b_tensor))
    return gamma_tiles, density.astype(jnp.bfloat16)
```

```python
import functools

import jax
import jax.numpy as jnp
from jax import lax
from jax.experimental import pallas as pl
from jax.experimental.pallas import tpu as pltpu
from jax.sharding import PartitionSpec as P

MESH = pl.DeviceIdType.MESH
PLUS, MINUS, ZED, SIBLING = range(4)
CHIPS_X, CHIPS_Z, CORES = 4, 2, 2
ROW = CHIPS_X * CHIPS_Z * CORES


def dot_nt(lhs, rhs):
    return lax.dot_general(lhs, rhs, (((1,), (1,)), ((), ())), preferred_element_type=jnp.float32)


def kernel(
    n_oi, b_hbm, occ_ref, dom_ref, pair_ref, pao_ref, gamma_out, dens_out,
    ball, bt, gsum, gout, gall, mcat, dacc, dpart, dall, small, vcol,
    link_send, piece_recv, small_send, small_recv, gam_send, gam_recv, den_send, den_recv, local_sem,
):
    naux, dom = b_hbm.shape[1], b_hbm.shape[2]
    blocks = dom // 128
    piece_rows = naux // 3
    slice_rows = naux // ROW
    strip = slice_rows // n_oi
    oi, oj = lax.axis_index("oi"), lax.axis_index("oj")
    core, x, z = lax.rem(oj, 2), lax.rem(oj // 2, CHIPS_X), oj // (CHIPS_X * CORES)

    def chip_at(dx, dz):
        return lax.rem(z + dz, CHIPS_Z) * CHIPS_X + lax.rem(x + dx, CHIPS_X)

    def place(dx, dz):
        return chip_at(dx, dz) * CORES + core

    sibling = oj + 1 - 2 * core
    link_to = {PLUS: place(1, 0), MINUS: place(3, 0), ZED: place(0, 1), SIBLING: sibling}
    first_owner = oj * n_oi
    my_slice = (oi * ROW + oj) // n_oi
    me = oi * ROW + oj
    self_owner = jnp.logical_and(first_owner <= me, me < first_owner + n_oi)

    def owner(t):
        flat = first_owner + t
        return flat // ROW, lax.rem(flat, ROW)

    barrier = pltpu.get_barrier_semaphore()
    for step in range(1, ROW):
        pl.semaphore_signal(barrier, inc=1, device_id=(oi, lax.rem(oj + step, ROW)), device_id_type=MESH)
    for t in range(n_oi):
        @pl.when(first_owner + t != me)
        def _():
            pl.semaphore_signal(barrier, inc=1, device_id=owner(t), device_id_type=MESH)

        @pl.when(jnp.logical_or(oi != t, oj != my_slice))
        def _():
            pl.semaphore_signal(barrier, inc=1, device_id=(t, my_slice), device_id_type=MESH)
    pl.semaphore_wait(barrier, ROW - 1 + 2 * n_oi - 2 * self_owner.astype(jnp.int32))

    counts = [0, 0, 0, 0]
    started = []

    def copy_of(slot, k, link, own=False):
        rows = pl.ds(k * piece_rows, piece_rows)
        copy = pltpu.make_async_remote_copy(
            src_ref=b_hbm.at[0, rows] if own else ball.at[slot, rows],
            dst_ref=ball.at[slot, rows],
            send_sem=link_send.at[link, counts[link]],
            recv_sem=piece_recv.at[slot, k],
            device_id=(oi, link_to[link]),
            device_id_type=MESH,
        )
        counts[link] += 1
        return copy

    def send(slot, k, link, own=False):
        copy = copy_of(slot, k, link, own)
        copy.start()
        started.append(copy)

    def wait_piece(slot, k):
        rows = pl.ds(k * piece_rows, piece_rows)
        pltpu.make_async_remote_copy(
            src_ref=ball.at[slot, rows],
            dst_ref=ball.at[slot, rows],
            send_sem=link_send.at[0, 0],
            recv_sem=piece_recv.at[slot, k],
            device_id=(oi, sibling),
            device_id_type=MESH,
        ).wait_recv()

    for k in range(3):
        for link in (PLUS, MINUS, ZED, SIBLING):
            send(oj, k, link, own=True)
    own_copy = pltpu.make_async_copy(b_hbm.at[0], ball.at[oj], local_sem.at[0])
    own_copy.start()

    lane = lax.broadcasted_iota(jnp.int32, (1, 128), 1)
    occupied = occ_ref[...].astype(jnp.float32)
    own_v = [pao_ref[pl.ds(dom_ref[0, k], 1), :] - occupied for k in range(blocks)]
    listed = jnp.zeros((1, 128), jnp.float32)
    for s in range(pair_ref.shape[1]):
        listed = listed + jnp.where(lane == pair_ref[0, s], 1.0, 0.0)
    small[oj] = jnp.concatenate(own_v + [listed] + [jnp.zeros((7 - blocks, 128), jnp.float32)], axis=0)

    def small_copy(step):
        target = lax.rem(oj + step, ROW)
        return pltpu.make_async_remote_copy(
            src_ref=small.at[oj],
            dst_ref=small.at[oj],
            send_sem=small_send.at[step],
            recv_sem=small_recv.at[step],
            device_id=(oi, target),
            device_id_type=MESH,
        )

    def small_arrival(step):
        source = lax.rem(oj + ROW - step, ROW)
        return pltpu.make_async_remote_copy(
            src_ref=small.at[source],
            dst_ref=small.at[source],
            send_sem=small_send.at[step],
            recv_sem=small_recv.at[step],
            device_id=(oi, source),
            device_id_type=MESH,
        )

    for step in range(1, ROW):
        small_copy(step).start()
    for k in range(blocks):
        vcol[k * 128:(k + 1) * 128, :] = jnp.transpose(jnp.broadcast_to(own_v[k], (128, 128)))
    own_copy.wait()
    for k in range(3):
        bt[:, k * piece_rows:(k + 1) * piece_rows] = jnp.transpose(ball[oj, k * piece_rows:(k + 1) * piece_rows, :])
    for step in range(1, ROW):
        small_arrival(step).wait_recv()

    half = dom // 2

    def amplitudes(partner, side):
        tile = small[partner]
        weight = jnp.sum(
            jnp.where(lane == partner, small[oj][blocks:blocks + 1], 0.0)
            + jnp.where(lane == oj, tile[blocks:blocks + 1], 0.0),
            axis=1, keepdims=True,
        )

        def part(h, carry):
            rows = pl.ds(pl.multiple_of(h * half, half), half)
            overlap = jnp.dot(bt[rows, :], ball[partner], preferred_element_type=jnp.float32)
            column = vcol[rows, :]
            denominator = jnp.concatenate([column + tile[k:k + 1] for k in range(blocks)], axis=1)
            mcat[rows, side * dom:(side + 1) * dom] = (overlap * (-weight) / denominator).astype(jnp.bfloat16)
            return carry

        lax.fori_loop(0, 2, part, 0)

    tile_rows = naux // 4
    per_tile = ROW // 4

    def update(chip, t):
        rows = pl.ds(pl.multiple_of(t * tile_rows, tile_rows), tile_rows)
        return rows, (
            dot_nt(ball[chip * CORES, rows, :], mcat[:, :dom])
            + dot_nt(ball[chip * CORES + 1, rows, :], mcat[:, dom:])
        )

    def process(chip, first=False):
        for side in range(CORES):
            amplitudes(chip * CORES + side, side)

        def step(t, carry):
            rows, term = update(chip, t)
            if first:
                gsum[rows, :] = term
            else:
                gsum[rows, :] += term
            return carry

        lax.fori_loop(0, 4, step, 0)

    def process_group(offsets):
        if len(offsets) == 1:
            process(chip_at(*offsets[0]))
            return

        def step(i, carry):
            chip = chip_at(*offsets[0])
            for n, offset in enumerate(offsets[1:]):
                chip = jnp.where(i == n + 1, chip_at(*offset), chip)
            process(chip)
            return carry

        lax.fori_loop(0, len(offsets), step, 0)

    def arrive(dx, dz, k):
        wait_piece(place(dx, dz), k)
        send(place(dx, dz), k, SIBLING)

    def arrived_at_sibling(dx, dz):
        other = chip_at(dx, dz) * CORES + 1 - core
        for k in range(3):
            wait_piece(other, k)

    arrived_at_sibling(0, 0)
    process(chip_at(0, 0), first=True)

    for dx, dz in ((3, 0), (1, 0), (0, 1)):
        arrive(dx, dz, 0)
    send(place(3, 0), 0, PLUS)
    send(place(3, 0), 0, ZED)
    send(place(1, 0), 0, ZED)
    for dx, dz in ((3, 0), (1, 0), (0, 1)):
        arrive(dx, dz, 1)
    send(place(0, 1), 1, PLUS)
    send(place(1, 0), 1, MINUS)
    send(place(1, 0), 1, ZED)
    for dx, dz in ((3, 0), (1, 0), (0, 1)):
        arrive(dx, dz, 2)
    send(place(0, 1), 2, PLUS)
    send(place(1, 0), 2, MINUS)
    send(place(0, 1), 2, MINUS)
    near = ((3, 0), (1, 0), (0, 1))
    for offset in near:
        arrived_at_sibling(*offset)
    process_group(near)

    arrive(2, 0, 0)
    send(place(2, 0), 0, ZED)
    arrive(2, 0, 1)
    arrive(3, 1, 0)
    arrive(3, 1, 1)
    send(place(3, 1), 1, PLUS)
    arrive(2, 0, 2)
    arrive(1, 1, 0)
    arrived_at_sibling(2, 0)
    process_group(((2, 0),))
    arrive(1, 1, 2)
    send(place(1, 1), 2, MINUS)
    arrive(3, 1, 2)
    arrive(1, 1, 1)
    diagonal = ((3, 1), (1, 1))
    for offset in diagonal:
        arrived_at_sibling(*offset)
    process_group(diagonal)
    for k in range(3):
        arrive(2, 1, k)
    arrived_at_sibling(2, 1)

    last = chip_at(2, 1)
    for side in range(CORES):
        amplitudes(last * CORES + side, side)

    def gamma_copy(target, source, where):
        return pltpu.make_async_remote_copy(
            src_ref=gout.at[pl.ds(pl.multiple_of(target * slice_rows, slice_rows), slice_rows)],
            dst_ref=gall.at[source],
            send_sem=gam_send.at[target],
            recv_sem=gam_recv.at[source],
            device_id=(oi, where),
            device_id_type=MESH,
        )

    own_slice = pltpu.make_async_copy(
        gout.at[pl.ds(pl.multiple_of(oj * slice_rows, slice_rows), slice_rows)], gall.at[oj], local_sem.at[1]
    )

    def out_copy(t):
        rows = pl.ds(pl.multiple_of(t * tile_rows, tile_rows), tile_rows)
        return pltpu.make_async_copy(gout.at[rows], gamma_out.at[0, rows], local_sem.at[2 + t])

    def finish(t, carry):
        rows, term = update(last, t)
        gout[rows, :] = (gsum[rows, :] + term).astype(jnp.bfloat16)
        out_copy(t).start()
        for k in range(per_tile):
            target = t * per_tile + k

            @pl.when(target != oj)
            def _():
                gamma_copy(target, oj, target).start()

            @pl.when(target == oj)
            def _():
                own_slice.start()
        return carry

    lax.fori_loop(0, 4, finish, 0)

    dacc[...] = jnp.zeros_like(dacc)

    def density(i, carry):
        source = (
            lax.rem(z + i // (CHIPS_X * CORES), CHIPS_Z) * CHIPS_X + lax.rem(x + i // CORES, CHIPS_X)
        ) * CORES + lax.rem(core + i, CORES)

        @pl.when(i == 0)
        def _():
            own_slice.wait()

        @pl.when(i > 0)
        def _():
            gamma_copy(source, source, source).wait_recv()

        dacc[...] += dot_nt(gall[source], ball[source])
        return carry

    lax.fori_loop(0, ROW, density, 0)
    for t in range(n_oi):
        dpart[t] = dacc[t * strip:(t + 1) * strip, :]

    def den_copy(t, row, where):
        return pltpu.make_async_remote_copy(
            src_ref=dpart.at[t],
            dst_ref=dall.at[row],
            send_sem=den_send.at[t],
            recv_sem=den_recv.at[row],
            device_id=where,
            device_id_type=MESH,
        )

    own_strip = me - first_owner

    def keep_copy():
        return pltpu.make_async_copy(dpart.at[jnp.clip(own_strip, 0, n_oi - 1)], dall.at[oi], local_sem.at[6])

    for t in range(n_oi):
        @pl.when(first_owner + t != me)
        def _():
            den_copy(t, oi, owner(t)).start()

    @pl.when(self_owner)
    def _():
        keep_copy().start()
        keep_copy().wait()

    for row in range(n_oi):
        @pl.when(jnp.logical_or(oi != row, oj != my_slice))
        def _():
            den_copy(0, row, (row, my_slice)).wait_recv()
    total = dall[0]
    for row in range(1, n_oi):
        total = total + dall[row]
    dens_out[...] = (total * (1.0 / (n_oi * ROW))).astype(jnp.bfloat16)

    for copy in started:
        copy.wait_send()
    for step in range(1, ROW):
        small_copy(step).wait_send()
    for t in range(4):
        out_copy(t).wait()

    def drain(target, carry):
        @pl.when(target != oj)
        def _():
            gamma_copy(target, oj, target).wait_send()
        return carry

    lax.fori_loop(0, ROW, drain, 0)
    for t in range(n_oi):
        @pl.when(first_owner + t != me)
        def _():
            den_copy(t, oi, owner(t)).wait_send()


def body(n_oi, b_tensor, occ_energy, dom_blocks, pair_cols, pao_energy):
    naux, dom = b_tensor.shape[1], b_tensor.shape[2]
    slice_rows = naux // ROW
    strip = slice_rows // n_oi
    vmem = pl.BlockSpec(memory_space=pltpu.VMEM)
    smem = pl.BlockSpec(memory_space=pltpu.SMEM)
    hbm = pl.BlockSpec(memory_space=pl.ANY)
    dma = pltpu.SemaphoreType.DMA
    return pl.pallas_call(
        functools.partial(kernel, n_oi),
        out_shape=(
            jax.ShapeDtypeStruct((1, naux, dom), jnp.bfloat16),
            jax.ShapeDtypeStruct((strip, naux), jnp.bfloat16),
        ),
        in_specs=[hbm, vmem, smem, smem, vmem],
        out_specs=(hbm, vmem),
        scratch_shapes=[
            pltpu.VMEM((ROW, naux, dom), jnp.bfloat16),
            pltpu.VMEM((dom, naux), jnp.bfloat16),
            pltpu.VMEM((naux, dom), jnp.float32),
            pltpu.VMEM((naux, dom), jnp.bfloat16),
            pltpu.VMEM((ROW, slice_rows, dom), jnp.bfloat16),
            pltpu.VMEM((dom, CORES * dom), jnp.bfloat16),
            pltpu.VMEM((slice_rows, naux), jnp.float32),
            pltpu.VMEM((n_oi, strip, naux), jnp.float32),
            pltpu.VMEM((n_oi, strip, naux), jnp.float32),
            pltpu.VMEM((ROW, 8, 128), jnp.float32),
            pltpu.VMEM((dom, 128), jnp.float32),
            dma((4, 24)),
            dma((ROW, 3)),
            dma((ROW,)),
            dma((ROW,)),
            dma((ROW,)),
            dma((ROW,)),
            dma((n_oi,)),
            dma((n_oi,)),
            dma((7,)),
        ],
        compiler_params=pltpu.CompilerParams(
            collective_id=0, has_side_effects=True, vmem_limit_bytes=56 * 2**20
        ),
        cost_estimate=pl.CostEstimate(
            flops=2 * naux * dom * dom * 32, bytes_accessed=4 * naux * dom, transcendentals=0
        ),
    )(b_tensor, occ_energy.reshape(1, 1), dom_blocks, pair_cols, pao_energy)


def solution(mesh):
    in_specs = (
        P(("oi", "oj"), None, None),
        P(("oi", "oj")),
        P(("oi", "oj"), None),
        P(("oi", "oj"), None),
        P(),
    )
    out_specs = (P(("oi", "oj"), None, None), P(("oi", "oj"), None))
    return jax.shard_map(
        functools.partial(body, mesh.shape["oi"]),
        mesh=mesh, in_specs=in_specs, out_specs=out_specs, check_vma=False,
    )
```

```python
import functools

import jax
import jax.numpy as jnp
from jax import lax
from jax.experimental import pallas as pl
from jax.experimental.pallas import tpu as pltpu
from jax.sharding import PartitionSpec as P

MESH = pl.DeviceIdType.MESH
PLUS, MINUS, ZED, SIBLING = range(4)
CHIPS_X, CHIPS_Z, CORES = 4, 2, 2
ROW = CHIPS_X * CHIPS_Z * CORES


def dot_nt(lhs, rhs):
    return lax.dot_general(lhs, rhs, (((1,), (1,)), ((), ())), preferred_element_type=jnp.float32)


def kernel(
    n_oi, b_hbm, occ_ref, dom_ref, pair_ref, pao_ref, gamma_out, dens_out,
    ball, bt, gsum, gout, gall, mcat, dacc, dpart, dall, small, vcol,
    link_send, piece_recv, small_send, small_recv, gam_send, gam_recv, den_send, den_recv, local_sem,
):
    naux, dom = b_hbm.shape[1], b_hbm.shape[2]
    blocks = dom // 128
    piece_rows = naux // 3
    slice_rows = naux // ROW
    strip = slice_rows // n_oi
    oi, oj = lax.axis_index("oi"), lax.axis_index("oj")
    core, x, z = lax.rem(oj, 2), lax.rem(oj // 2, CHIPS_X), oj // (CHIPS_X * CORES)

    def chip_at(dx, dz):
        return lax.rem(z + dz, CHIPS_Z) * CHIPS_X + lax.rem(x + dx, CHIPS_X)

    def place(dx, dz):
        return chip_at(dx, dz) * CORES + core

    sibling = oj + 1 - 2 * core
    link_to = {PLUS: place(1, 0), MINUS: place(3, 0), ZED: place(0, 1), SIBLING: sibling}
    first_owner = oj * n_oi
    my_slice = (oi * ROW + oj) // n_oi
    me = oi * ROW + oj
    self_owner = jnp.logical_and(first_owner <= me, me < first_owner + n_oi)

    def owner(t):
        flat = first_owner + t
        return flat // ROW, lax.rem(flat, ROW)

    barrier = pltpu.get_barrier_semaphore()
    for step in range(1, ROW):
        pl.semaphore_signal(barrier, inc=1, device_id=(oi, lax.rem(oj + step, ROW)), device_id_type=MESH)
    for t in range(n_oi):
        @pl.when(first_owner + t != me)
        def _():
            pl.semaphore_signal(barrier, inc=1, device_id=owner(t), device_id_type=MESH)

        @pl.when(jnp.logical_or(oi != t, oj != my_slice))
        def _():
            pl.semaphore_signal(barrier, inc=1, device_id=(t, my_slice), device_id_type=MESH)
    pl.semaphore_wait(barrier, ROW - 1 + 2 * n_oi - 2 * self_owner.astype(jnp.int32))

    counts = [0, 0, 0, 0]
    started = []

    def copy_of(slot, k, link, own=False):
        rows = pl.ds(k * piece_rows, piece_rows)
        copy = pltpu.make_async_remote_copy(
            src_ref=b_hbm.at[0, rows] if own else ball.at[slot, rows],
            dst_ref=ball.at[slot, rows],
            send_sem=link_send.at[link, counts[link]],
            recv_sem=piece_recv.at[slot, k],
            device_id=(oi, link_to[link]),
            device_id_type=MESH,
        )
        counts[link] += 1
        return copy

    def send(slot, k, link, own=False):
        copy = copy_of(slot, k, link, own)
        copy.start()
        started.append(copy)

    def wait_piece(slot, k):
        rows = pl.ds(k * piece_rows, piece_rows)
        pltpu.make_async_remote_copy(
            src_ref=ball.at[slot, rows],
            dst_ref=ball.at[slot, rows],
            send_sem=link_send.at[0, 0],
            recv_sem=piece_recv.at[slot, k],
            device_id=(oi, sibling),
            device_id_type=MESH,
        ).wait_recv()

    for k in range(3):
        for link in (PLUS, MINUS, ZED, SIBLING):
            send(oj, k, link, own=True)
    own_copy = pltpu.make_async_copy(b_hbm.at[0], ball.at[oj], local_sem.at[0])
    own_copy.start()

    lane = lax.broadcasted_iota(jnp.int32, (1, 128), 1)
    occupied = occ_ref[...].astype(jnp.float32)
    own_v = [pao_ref[pl.ds(dom_ref[0, k], 1), :] - occupied for k in range(blocks)]
    listed = jnp.zeros((1, 128), jnp.float32)
    for s in range(pair_ref.shape[1]):
        listed = listed + jnp.where(lane == pair_ref[0, s], 1.0, 0.0)
    small[oj] = jnp.concatenate(own_v + [listed] + [jnp.zeros((7 - blocks, 128), jnp.float32)], axis=0)

    def small_copy(step):
        target = lax.rem(oj + step, ROW)
        return pltpu.make_async_remote_copy(
            src_ref=small.at[oj],
            dst_ref=small.at[oj],
            send_sem=small_send.at[step],
            recv_sem=small_recv.at[step],
            device_id=(oi, target),
            device_id_type=MESH,
        )

    def small_arrival(step):
        source = lax.rem(oj + ROW - step, ROW)
        return pltpu.make_async_remote_copy(
            src_ref=small.at[source],
            dst_ref=small.at[source],
            send_sem=small_send.at[step],
            recv_sem=small_recv.at[step],
            device_id=(oi, source),
            device_id_type=MESH,
        )

    for step in range(1, ROW):
        small_copy(step).start()
    for k in range(blocks):
        vcol[k * 128:(k + 1) * 128, :] = jnp.transpose(jnp.broadcast_to(own_v[k], (128, 128)))
    own_copy.wait()
    for k in range(3):
        bt[:, k * piece_rows:(k + 1) * piece_rows] = jnp.transpose(ball[oj, k * piece_rows:(k + 1) * piece_rows, :])
    for step in range(1, ROW):
        small_arrival(step).wait_recv()

    half = dom // 2

    def amplitudes(partner, side):
        tile = small[partner]
        weight = jnp.sum(
            jnp.where(lane == partner, small[oj][blocks:blocks + 1], 0.0)
            + jnp.where(lane == oj, tile[blocks:blocks + 1], 0.0),
            axis=1, keepdims=True,
        )

        def part(h, carry):
            rows = pl.ds(pl.multiple_of(h * half, half), half)
            overlap = jnp.dot(bt[rows, :], ball[partner], preferred_element_type=jnp.float32)
            column = vcol[rows, :]
            denominator = jnp.concatenate([column + tile[k:k + 1] for k in range(blocks)], axis=1)
            mcat[rows, side * dom:(side + 1) * dom] = (overlap * (-weight) / denominator).astype(jnp.bfloat16)
            return carry

        lax.fori_loop(0, 2, part, 0)

    tile_rows = naux // 4
    chips = ROW // CORES
    chip_rows = naux // chips
    ring = ((2, 1), (1, 1), (3, 1), (2, 0), (0, 1), (1, 0), (3, 0), (0, 0))

    def pick(i, offsets):
        chip = chip_at(*offsets[0])
        for n, offset in enumerate(offsets[1:]):
            chip = jnp.where(i == n + 1, chip_at(*offset), chip)
        return chip

    def update(chip, t, size=tile_rows):
        rows = pl.ds(pl.multiple_of(t * size, size), size)
        return rows, (
            dot_nt(ball[chip * CORES, rows, :], mcat[:, :dom])
            + dot_nt(ball[chip * CORES + 1, rows, :], mcat[:, dom:])
        )

    def process(chip, first=False):
        for side in range(CORES):
            amplitudes(chip * CORES + side, side)

        def step(t, carry):
            rows, term = update(chip, t)
            if first:
                gsum[rows, :] = term
            else:
                gsum[rows, :] += term
            return carry

        lax.fori_loop(0, 4, step, 0)

    def process_group(offsets):
        if len(offsets) == 1:
            process(chip_at(*offsets[0]))
            return

        def step(i, carry):
            process(pick(i, offsets))
            return carry

        lax.fori_loop(0, len(offsets), step, 0)

    def arrive(dx, dz, k):
        wait_piece(place(dx, dz), k)
        send(place(dx, dz), k, SIBLING)

    def arrived_at_sibling(dx, dz):
        other = chip_at(dx, dz) * CORES + 1 - core
        for k in range(3):
            wait_piece(other, k)

    arrived_at_sibling(0, 0)
    process(chip_at(0, 0), first=True)

    for dx, dz in ((3, 0), (1, 0), (0, 1)):
        arrive(dx, dz, 0)
    send(place(3, 0), 0, PLUS)
    send(place(3, 0), 0, ZED)
    send(place(1, 0), 0, ZED)
    for dx, dz in ((3, 0), (1, 0), (0, 1)):
        arrive(dx, dz, 1)
    send(place(0, 1), 1, PLUS)
    send(place(1, 0), 1, MINUS)
    send(place(1, 0), 1, ZED)
    for dx, dz in ((3, 0), (1, 0), (0, 1)):
        arrive(dx, dz, 2)
    send(place(0, 1), 2, PLUS)
    send(place(1, 0), 2, MINUS)
    send(place(0, 1), 2, MINUS)
    near = ((3, 0), (1, 0), (0, 1))
    for offset in near:
        arrived_at_sibling(*offset)
    process_group(near)

    arrive(2, 0, 0)
    send(place(2, 0), 0, ZED)
    arrive(2, 0, 1)
    arrive(3, 1, 0)
    arrive(3, 1, 1)
    send(place(3, 1), 1, PLUS)
    arrive(2, 0, 2)
    arrive(1, 1, 0)
    arrived_at_sibling(2, 0)
    process_group(((2, 0),))
    arrive(1, 1, 2)
    send(place(1, 1), 2, MINUS)
    arrive(3, 1, 2)
    arrive(1, 1, 1)
    diagonal = ((3, 1), (1, 1))
    for offset in diagonal:
        arrived_at_sibling(*offset)
    process_group(diagonal)
    for k in range(3):
        arrive(2, 1, k)
    arrived_at_sibling(2, 1)

    last = chip_at(2, 1)
    for side in range(CORES):
        amplitudes(last * CORES + side, side)

    def gamma_copy(target, source, where):
        return pltpu.make_async_remote_copy(
            src_ref=gout.at[pl.ds(pl.multiple_of(target * slice_rows, slice_rows), slice_rows)],
            dst_ref=gall.at[source],
            send_sem=gam_send.at[target],
            recv_sem=gam_recv.at[source],
            device_id=(oi, where),
            device_id_type=MESH,
        )

    own_slice = pltpu.make_async_copy(
        gout.at[pl.ds(pl.multiple_of(oj * slice_rows, slice_rows), slice_rows)], gall.at[oj], local_sem.at[1]
    )

    def out_copy(t):
        rows = pl.ds(pl.multiple_of(t * chip_rows, chip_rows), chip_rows)
        return pltpu.make_async_copy(gout.at[rows], gamma_out.at[0, rows], local_sem.at[3 + t])

    def finish(i, carry):
        chip = pick(i, ring)
        rows, term = update(last, chip, chip_rows)
        gout[rows, :] = (gsum[rows, :] + term).astype(jnp.bfloat16)
        out_copy(chip).start()
        for k in range(CORES):
            target = chip * CORES + lax.rem(core + k, CORES)

            @pl.when(target != oj)
            def _():
                gamma_copy(target, oj, target).start()

            @pl.when(target == oj)
            def _():
                own_slice.start()
        return carry

    lax.fori_loop(0, chips, finish, 0)

    dacc[...] = jnp.zeros_like(dacc)

    def density(i, carry):
        source = pick(i // CORES, ring) * CORES + lax.rem(core + i, CORES)

        @pl.when(source == oj)
        def _():
            own_slice.wait()

        @pl.when(source != oj)
        def _():
            gamma_copy(source, source, source).wait_recv()

        dacc[...] += dot_nt(gall[source], ball[source])
        return carry

    lax.fori_loop(0, ROW, density, 0)
    groups = 4
    lanes = naux // groups
    for t in range(n_oi):
        rows = dacc[t * strip:(t + 1) * strip, :]
        dpart[t] = jnp.concatenate(
            [rows[:, g * lanes:(g + 1) * lanes] for g in range(groups)], axis=0
        ).astype(jnp.bfloat16)

    def den_copy(t, row, where):
        return pltpu.make_async_remote_copy(
            src_ref=dpart.at[t],
            dst_ref=dall.at[row],
            send_sem=den_send.at[t],
            recv_sem=den_recv.at[row],
            device_id=where,
            device_id_type=MESH,
        )

    own_strip = me - first_owner

    def keep_copy():
        return pltpu.make_async_copy(dpart.at[jnp.clip(own_strip, 0, n_oi - 1)], dall.at[oi], local_sem.at[2])

    for t in range(n_oi):
        @pl.when(first_owner + t != me)
        def _():
            den_copy(t, oi, owner(t)).start()

    @pl.when(self_owner)
    def _():
        keep_copy().start()
        keep_copy().wait()

    for row in range(n_oi):
        @pl.when(jnp.logical_or(oi != row, oj != my_slice))
        def _():
            den_copy(0, row, (row, my_slice)).wait_recv()
    total = dall[0].astype(jnp.float32)
    for row in range(1, n_oi):
        total = total + dall[row].astype(jnp.float32)
    total = total * (1.0 / (n_oi * ROW))
    dens_out[...] = jnp.concatenate(
        [total[g * strip:(g + 1) * strip] for g in range(groups)], axis=1
    ).astype(jnp.bfloat16)

    for copy in started:
        copy.wait_send()
    for step in range(1, ROW):
        small_copy(step).wait_send()
    for t in range(chips):
        out_copy(t).wait()

    def drain(target, carry):
        @pl.when(target != oj)
        def _():
            gamma_copy(target, oj, target).wait_send()
        return carry

    lax.fori_loop(0, ROW, drain, 0)
    for t in range(n_oi):
        @pl.when(first_owner + t != me)
        def _():
            den_copy(t, oi, owner(t)).wait_send()


def body(n_oi, b_tensor, occ_energy, dom_blocks, pair_cols, pao_energy):
    naux, dom = b_tensor.shape[1], b_tensor.shape[2]
    slice_rows = naux // ROW
    strip = slice_rows // n_oi
    vmem = pl.BlockSpec(memory_space=pltpu.VMEM)
    smem = pl.BlockSpec(memory_space=pltpu.SMEM)
    hbm = pl.BlockSpec(memory_space=pl.ANY)
    dma = pltpu.SemaphoreType.DMA
    return pl.pallas_call(
        functools.partial(kernel, n_oi),
        out_shape=(
            jax.ShapeDtypeStruct((1, naux, dom), jnp.bfloat16),
            jax.ShapeDtypeStruct((strip, naux), jnp.bfloat16),
        ),
        in_specs=[hbm, vmem, smem, smem, vmem],
        out_specs=(hbm, vmem),
        scratch_shapes=[
            pltpu.VMEM((ROW, naux, dom), jnp.bfloat16),
            pltpu.VMEM((dom, naux), jnp.bfloat16),
            pltpu.VMEM((naux, dom), jnp.float32),
            pltpu.VMEM((naux, dom), jnp.bfloat16),
            pltpu.VMEM((ROW, slice_rows, dom), jnp.bfloat16),
            pltpu.VMEM((dom, CORES * dom), jnp.bfloat16),
            pltpu.VMEM((slice_rows, naux), jnp.float32),
            pltpu.VMEM((n_oi, 4 * strip, naux // 4), jnp.bfloat16),
            pltpu.VMEM((n_oi, 4 * strip, naux // 4), jnp.bfloat16),
            pltpu.VMEM((ROW, 8, 128), jnp.float32),
            pltpu.VMEM((dom, 128), jnp.float32),
            dma((4, 24)),
            dma((ROW, 3)),
            dma((ROW,)),
            dma((ROW,)),
            dma((ROW,)),
            dma((ROW,)),
            dma((n_oi,)),
            dma((n_oi,)),
            dma((11,)),
        ],
        compiler_params=pltpu.CompilerParams(
            collective_id=0, has_side_effects=True, vmem_limit_bytes=56 * 2**20
        ),
        cost_estimate=pl.CostEstimate(
            flops=2 * naux * dom * dom * 32, bytes_accessed=4 * naux * dom, transcendentals=0
        ),
    )(b_tensor, occ_energy.reshape(1, 1), dom_blocks, pair_cols, pao_energy)


def solution(mesh):
    in_specs = (
        P(("oi", "oj"), None, None),
        P(("oi", "oj")),
        P(("oi", "oj"), None),
        P(("oi", "oj"), None),
        P(),
    )
    out_specs = (P(("oi", "oj"), None, None), P(("oi", "oj"), None))
    return jax.shard_map(
        functools.partial(body, mesh.shape["oi"]),
        mesh=mesh, in_specs=in_specs, out_specs=out_specs, check_vma=False,
    )
```

```python
import functools

import jax
import jax.numpy as jnp
from jax import lax
from jax.experimental import pallas as pl
from jax.experimental.pallas import tpu as pltpu
from jax.sharding import PartitionSpec as P

MESH = pl.DeviceIdType.MESH
PLUS, MINUS, ZED, SIBLING = range(4)
CHIPS_X, CHIPS_Z, CORES = 4, 2, 2
ROW = CHIPS_X * CHIPS_Z * CORES
HEAD = 16


def dot_nt(lhs, rhs):
    return lax.dot_general(lhs, rhs, (((1,), (1,)), ((), ())), preferred_element_type=jnp.float32)


def kernel(
    n_oi, b_hbm, occ_ref, dom_ref, pair_ref, pao_ref, gamma_out, dens_out,
    ball, bt, gsum, gout, gall, mcat, dacc, dpart, dall, vcol,
    link_send, piece_recv, gam_send, gam_recv, den_send, den_recv, local_sem, known,
):
    naux, dom = b_hbm.shape[1], b_hbm.shape[2]
    blocks = dom // 128
    piece_rows = naux // 3
    slice_rows = naux // ROW
    strip = slice_rows // n_oi
    oi, oj = lax.axis_index("oi"), lax.axis_index("oj")
    core, x, z = lax.rem(oj, 2), lax.rem(oj // 2, CHIPS_X), oj // (CHIPS_X * CORES)

    def chip_at(dx, dz):
        return lax.rem(z + dz, CHIPS_Z) * CHIPS_X + lax.rem(x + dx, CHIPS_X)

    def place(dx, dz):
        return chip_at(dx, dz) * CORES + core

    sibling = oj + 1 - 2 * core
    link_to = {PLUS: place(1, 0), MINUS: place(3, 0), ZED: place(0, 1), SIBLING: sibling}

    def slice_of(position):
        return (
            lax.rem(position // CORES, CHIPS_X) * (CORES * CHIPS_Z)
            + lax.rem(position, CORES) * CHIPS_Z
            + position // (CHIPS_X * CORES)
        )

    def position_of(part):
        return (
            lax.rem(part, CHIPS_Z) * CHIPS_X + part // (CORES * CHIPS_Z)
        ) * CORES + lax.rem(part // CHIPS_Z, CORES)

    me = oi * ROW + oj
    first_owner = slice_of(oj) * n_oi
    my_slice = position_of(me // n_oi)
    self_owner = jnp.logical_and(first_owner <= me, me < first_owner + n_oi)

    def owner(t):
        flat = first_owner + t
        return flat // ROW, lax.rem(flat, ROW)

    own_copy = pltpu.make_async_copy(b_hbm.at[0], ball.at[oj, pl.ds(HEAD, naux)], local_sem.at[0])
    own_copy.start()

    lane = lax.broadcasted_iota(jnp.int32, (1, dom), 1)
    occupied = occ_ref[...].astype(jnp.float32)
    own_v = [pao_ref[pl.ds(dom_ref[0, k], 1), :] - occupied for k in range(blocks)]
    rest = jnp.concatenate(own_v, axis=1)
    head = []
    for _ in range(3):
        head.append(rest.astype(jnp.bfloat16).astype(jnp.float32))
        rest = rest - head[-1]
    listed = jnp.zeros((1, dom), jnp.float32)
    for s in range(pair_ref.shape[1]):
        listed = listed + jnp.where(lane == pair_ref[0, s], 1.0, 0.0)
    head += [listed, jnp.zeros((HEAD - 4, dom), jnp.float32)]
    ball[oj, 0:HEAD, :] = jnp.concatenate(head, axis=0).astype(jnp.bfloat16)
    own_copy.wait()

    y_index, z_high = oi // 2, lax.rem(oi, 2)
    beside = [(oi, link_to[link]) for link in range(4)]
    rows_beside = [
        (lax.rem(y_index + 1, 4) * 2 + z_high, oj),
        (lax.rem(y_index + 3, 4) * 2 + z_high, oj),
        (oi + 1 - 2 * z_high, oj),
    ]
    barrier = pltpu.get_barrier_semaphore()
    for device in beside + rows_beside:
        pl.semaphore_signal(barrier, inc=1, device_id=device, device_id_type=MESH)
    pl.semaphore_wait(barrier, len(beside + rows_beside))

    def tell(stage):
        for device in rows_beside:
            pl.semaphore_signal(known.at[stage], inc=1, device_id=device, device_id_type=MESH)

    def hear(stage):
        pl.semaphore_wait(known.at[stage], len(rows_beside))

    counts = [0, 0, 0, 0]
    started = []

    def piece(slot, k):
        if k == 0:
            return ball.at[slot, pl.ds(0, HEAD + piece_rows)]
        return ball.at[slot, pl.ds(HEAD + k * piece_rows, piece_rows)]

    def send(slot, k, link):
        copy = pltpu.make_async_remote_copy(
            src_ref=piece(slot, k),
            dst_ref=piece(slot, k),
            send_sem=link_send.at[link, counts[link]],
            recv_sem=piece_recv.at[slot, k],
            device_id=(oi, link_to[link]),
            device_id_type=MESH,
        )
        counts[link] += 1
        copy.start()
        started.append(copy)

    def wait_piece(slot, k):
        pltpu.make_async_remote_copy(
            src_ref=piece(slot, k),
            dst_ref=piece(slot, k),
            send_sem=link_send.at[0, 0],
            recv_sem=piece_recv.at[slot, k],
            device_id=(oi, sibling),
            device_id_type=MESH,
        ).wait_recv()

    for k in range(3):
        for link in (PLUS, MINUS, ZED, SIBLING):
            send(oj, k, link)

    for k in range(blocks):
        vcol[k * 128:(k + 1) * 128, :] = jnp.transpose(jnp.broadcast_to(own_v[k], (128, 128)))
    for k in range(3):
        bt[:, k * piece_rows:(k + 1) * piece_rows] = jnp.transpose(
            ball[oj, HEAD + k * piece_rows:HEAD + (k + 1) * piece_rows, :]
        )

    def block(slot, start=0, size=naux):
        return ball[slot, pl.ds(pl.multiple_of(HEAD + start, HEAD), size), :]

    def amplitudes(partner, side):
        own_head = ball[oj, 0:HEAD, :].astype(jnp.float32)
        its_head = ball[partner, 0:HEAD, :].astype(jnp.float32)
        energies = its_head[0:1] + its_head[1:2] + its_head[2:3]
        weight = jnp.sum(
            jnp.where(lane == partner, own_head[3:4], 0.0) + jnp.where(lane == oj, its_head[3:4], 0.0),
            axis=1, keepdims=True,
        )
        overlap = jnp.dot(bt[...], block(partner), preferred_element_type=jnp.float32)
        column = vcol[...]
        denominator = jnp.concatenate(
            [column + energies[:, k * 128:(k + 1) * 128] for k in range(blocks)], axis=1
        )
        mcat[:, pl.ds(pl.multiple_of(side * dom, dom), dom)] = (
            overlap * (-weight) / denominator
        ).astype(jnp.bfloat16)

    half_rows = naux // 2

    def pick(i, offsets):
        chip = chip_at(*offsets[0])
        for n, offset in enumerate(offsets[1:]):
            chip = jnp.where(i == n + 1, chip_at(*offset), chip)
        return chip

    def update(chip, start=0, size=naux):
        return (
            dot_nt(block(chip * CORES, start, size), mcat[:, :dom])
            + dot_nt(block(chip * CORES + 1, start, size), mcat[:, dom:])
        )

    def process(chip, first=False):
        for side in range(CORES):
            amplitudes(chip * CORES + side, side)

        if first:
            gsum[...] = update(chip)
        else:
            gsum[...] += update(chip)

    def process_group(offsets):
        if len(offsets) == 1:
            process(chip_at(*offsets[0]))
            return

        def step(i, carry):
            process(pick(i, offsets))
            return carry

        lax.fori_loop(0, len(offsets), step, 0)

    def arrive(dx, dz, k):
        wait_piece(place(dx, dz), k)
        send(place(dx, dz), k, SIBLING)

    def arrived_at_sibling(dx, dz):
        other = chip_at(dx, dz) * CORES + 1 - core
        for k in range(3):
            wait_piece(other, k)

    arrived_at_sibling(0, 0)
    process(chip_at(0, 0), first=True)

    for dx, dz in ((3, 0), (1, 0), (0, 1)):
        arrive(dx, dz, 0)
    send(place(3, 0), 0, PLUS)
    send(place(3, 0), 0, ZED)
    send(place(1, 0), 0, ZED)
    for dx, dz in ((3, 0), (1, 0), (0, 1)):
        arrive(dx, dz, 1)
    send(place(0, 1), 1, PLUS)
    send(place(1, 0), 1, MINUS)
    send(place(1, 0), 1, ZED)
    for dx, dz in ((3, 0), (1, 0), (0, 1)):
        arrive(dx, dz, 2)
    send(place(0, 1), 2, PLUS)
    send(place(1, 0), 2, MINUS)
    send(place(0, 1), 2, MINUS)
    near = ((3, 0), (1, 0), (0, 1))
    for offset in near:
        arrived_at_sibling(*offset)
    process_group(near)

    arrive(2, 0, 0)
    send(place(2, 0), 0, ZED)
    arrive(2, 0, 1)
    arrive(3, 1, 0)
    arrive(3, 1, 1)
    send(place(3, 1), 1, PLUS)
    arrive(2, 0, 2)
    arrive(1, 1, 0)
    arrived_at_sibling(2, 0)
    process_group(((2, 0),))
    arrive(1, 1, 2)
    send(place(1, 1), 2, MINUS)
    arrive(3, 1, 2)
    arrive(1, 1, 1)
    diagonal = ((3, 1), (1, 1))
    for offset in diagonal:
        arrived_at_sibling(*offset)
    process_group(diagonal)
    last = chip_at(2, 1)
    for k in range(3):
        arrive(2, 1, k)

    amplitudes(last * CORES + core, core)
    arrived_at_sibling(2, 1)
    tell(0)
    amplitudes(last * CORES + 1 - core, 1 - core)

    def slice_rows_of(position):
        return pl.ds(pl.multiple_of(slice_of(position) * slice_rows, slice_rows), slice_rows)

    def gamma_copy(target, source, where):
        return pltpu.make_async_remote_copy(
            src_ref=gout.at[slice_rows_of(target)],
            dst_ref=gall.at[source],
            send_sem=gam_send.at[target],
            recv_sem=gam_recv.at[source],
            device_id=(oi, where),
            device_id_type=MESH,
        )

    own_slice = pltpu.make_async_copy(gout.at[slice_rows_of(oj)], gall.at[oj], local_sem.at[1])

    def out_copy(i):
        rows = pl.ds(pl.multiple_of(i * half_rows, half_rows), half_rows)
        return pltpu.make_async_copy(gout.at[rows], gamma_out.at[0, rows], local_sem.at[3 + i])

    ring = ((2, 1), (2, 0), (1, 1), (3, 1), (1, 0), (3, 0), (0, 1), (0, 0))

    def finish(i, carry):
        part = lax.rem(x // 2 + 1 + i, 2)
        rows = pl.ds(pl.multiple_of(part * half_rows, half_rows), half_rows)
        term = update(last, part * half_rows, half_rows)
        gout[rows, :] = (gsum[rows, :] + term).astype(jnp.bfloat16)

        def leave(n, inner):
            chip = pick(n, ring)
            for k in range(CORES):
                target = chip * CORES + lax.rem(core + k, CORES)
                here = lax.rem(chip, CHIPS_X) // 2 == part

                @pl.when(jnp.logical_and(here, target != oj))
                def _():
                    gamma_copy(target, oj, target).start()

                @pl.when(jnp.logical_and(here, target == oj))
                def _():
                    own_slice.start()
            return inner

        lax.fori_loop(0, ROW // CORES, leave, 0)
        out_copy(part).start()
        return carry

    lax.fori_loop(0, 2, finish, 0)
    hear(0)
    tell(1)

    dacc[...] = jnp.zeros_like(dacc)

    def density(i, carry):
        chip = pick(i, ring)
        for k in range(CORES):
            source = chip * CORES + k

            @pl.when(source == oj)
            def _():
                own_slice.wait()

            @pl.when(source != oj)
            def _():
                gamma_copy(source, source, source).wait_recv()

        source = chip * CORES
        dacc[...] += (
            dot_nt(gall[source], block(source)) + dot_nt(gall[source + 1], block(source + 1))
        )
        return carry

    lax.fori_loop(0, 3, density, 0)
    hear(1)
    tell(2)
    lax.fori_loop(3, ROW // CORES, density, 0)
    hear(2)
    groups = 4
    lanes = naux // groups
    for t in range(n_oi):
        rows = dacc[t * strip:(t + 1) * strip, :]
        dpart[t] = jnp.concatenate(
            [rows[:, g * lanes:(g + 1) * lanes] for g in range(groups)], axis=0
        ).astype(jnp.bfloat16)

    def den_copy(t, row, where):
        return pltpu.make_async_remote_copy(
            src_ref=dpart.at[t],
            dst_ref=dall.at[row],
            send_sem=den_send.at[t],
            recv_sem=den_recv.at[row],
            device_id=where,
            device_id_type=MESH,
        )

    own_strip = me - first_owner

    def keep_copy():
        return pltpu.make_async_copy(dpart.at[jnp.clip(own_strip, 0, n_oi - 1)], dall.at[oi], local_sem.at[2])

    for t in range(n_oi):
        @pl.when(first_owner + t != me)
        def _():
            den_copy(t, oi, owner(t)).start()

    @pl.when(self_owner)
    def _():
        keep_copy().start()
        keep_copy().wait()

    for row in range(n_oi):
        @pl.when(jnp.logical_or(oi != row, oj != my_slice))
        def _():
            den_copy(0, row, (row, my_slice)).wait_recv()
    total = dall[0].astype(jnp.float32)
    for row in range(1, n_oi):
        total = total + dall[row].astype(jnp.float32)
    total = total * (1.0 / (n_oi * ROW))
    dens_out[...] = jnp.concatenate(
        [total[g * strip:(g + 1) * strip] for g in range(groups)], axis=1
    ).astype(jnp.bfloat16)

    for copy in started:
        copy.wait_send()
    for t in range(2):
        out_copy(t).wait()

    def drain(target, carry):
        @pl.when(target != oj)
        def _():
            gamma_copy(target, oj, target).wait_send()
        return carry

    lax.fori_loop(0, ROW, drain, 0)
    for t in range(n_oi):
        @pl.when(first_owner + t != me)
        def _():
            den_copy(t, oi, owner(t)).wait_send()


def body(n_oi, b_tensor, occ_energy, dom_blocks, pair_cols, pao_energy):
    naux, dom = b_tensor.shape[1], b_tensor.shape[2]
    slice_rows = naux // ROW
    strip = slice_rows // n_oi
    vmem = pl.BlockSpec(memory_space=pltpu.VMEM)
    smem = pl.BlockSpec(memory_space=pltpu.SMEM)
    hbm = pl.BlockSpec(memory_space=pl.ANY)
    dma = pltpu.SemaphoreType.DMA
    return pl.pallas_call(
        functools.partial(kernel, n_oi),
        out_shape=(
            jax.ShapeDtypeStruct((1, naux, dom), jnp.bfloat16),
            jax.ShapeDtypeStruct((strip, naux), jnp.bfloat16),
        ),
        in_specs=[hbm, vmem, smem, smem, vmem],
        out_specs=(hbm, vmem),
        scratch_shapes=[
            pltpu.VMEM((ROW, HEAD + naux, dom), jnp.bfloat16),
            pltpu.VMEM((dom, naux), jnp.bfloat16),
            pltpu.VMEM((naux, dom), jnp.float32),
            pltpu.VMEM((naux, dom), jnp.bfloat16),
            pltpu.VMEM((ROW, slice_rows, dom), jnp.bfloat16),
            pltpu.VMEM((dom, CORES * dom), jnp.bfloat16),
            pltpu.VMEM((slice_rows, naux), jnp.float32),
            pltpu.VMEM((n_oi, 4 * strip, naux // 4), jnp.bfloat16),
            pltpu.VMEM((n_oi, 4 * strip, naux // 4), jnp.bfloat16),
            pltpu.VMEM((dom, 128), jnp.float32),
            dma((4, 24)),
            dma((ROW, 3)),
            dma((ROW,)),
            dma((ROW,)),
            dma((n_oi,)),
            dma((n_oi,)),
            dma((5,)),
            pltpu.SemaphoreType.REGULAR((3,)),
        ],
        compiler_params=pltpu.CompilerParams(
            collective_id=0, has_side_effects=True, vmem_limit_bytes=56 * 2**20
        ),
        cost_estimate=pl.CostEstimate(
            flops=2 * naux * dom * dom * 32, bytes_accessed=4 * naux * dom, transcendentals=0
        ),
    )(b_tensor, occ_energy.reshape(1, 1), dom_blocks, pair_cols, pao_energy)


def solution(mesh):
    in_specs = (
        P(("oi", "oj"), None, None),
        P(("oi", "oj")),
        P(("oi", "oj"), None),
        P(("oi", "oj"), None),
        P(),
    )
    out_specs = (P(("oi", "oj"), None, None), P(("oi", "oj"), None))
    return jax.shard_map(
        functools.partial(body, mesh.shape["oi"]),
        mesh=mesh, in_specs=in_specs, out_specs=out_specs, check_vma=False,
    )
```

```python
import functools

import jax
import jax.numpy as jnp
from jax import lax
from jax.experimental import pallas as pl
from jax.experimental.pallas import tpu as pltpu
from jax.sharding import PartitionSpec as P

MESH = pl.DeviceIdType.MESH
PLUS, MINUS, ZED, SIBLING = range(4)
CHIPS_X, CHIPS_Z, CORES = 4, 2, 2
ROW = CHIPS_X * CHIPS_Z * CORES
HEAD = 16


def dot_nt(lhs, rhs):
    return lax.dot_general(lhs, rhs, (((1,), (1,)), ((), ())), preferred_element_type=jnp.float32)


def kernel(
    n_oi, b_hbm, occ_ref, dom_ref, pair_ref, pao_ref, gamma_out, dens_out,
    ball, bt, gsum, gout, gall, mcat, dacc, dpart, dall, vcol,
    link_send, piece_recv, gam_send, gam_recv, den_send, den_recv, local_sem, known,
):
    naux, dom = b_hbm.shape[1], b_hbm.shape[2]
    blocks = dom // 128
    piece_rows = naux // 3
    slice_rows = naux // ROW
    strip = slice_rows // n_oi
    oi, oj = lax.axis_index("oi"), lax.axis_index("oj")
    core, x, z = lax.rem(oj, 2), lax.rem(oj // 2, CHIPS_X), oj // (CHIPS_X * CORES)

    def chip_at(dx, dz):
        return lax.rem(z + dz, CHIPS_Z) * CHIPS_X + lax.rem(x + dx, CHIPS_X)

    def place(dx, dz):
        return chip_at(dx, dz) * CORES + core

    sibling = oj + 1 - 2 * core
    link_to = {PLUS: place(1, 0), MINUS: place(3, 0), ZED: place(0, 1), SIBLING: sibling}

    def slice_of(position):
        return (
            lax.rem(position // CORES, CHIPS_X) * (CORES * CHIPS_Z)
            + lax.rem(position, CORES) * CHIPS_Z
            + position // (CHIPS_X * CORES)
        )

    def position_of(part):
        return (
            lax.rem(part, CHIPS_Z) * CHIPS_X + part // (CORES * CHIPS_Z)
        ) * CORES + lax.rem(part // CHIPS_Z, CORES)

    me = oi * ROW + oj
    first_owner = slice_of(oj) * n_oi
    my_slice = position_of(me // n_oi)
    self_owner = jnp.logical_and(first_owner <= me, me < first_owner + n_oi)

    def owner(t):
        flat = first_owner + t
        return flat // ROW, lax.rem(flat, ROW)

    y_index, z_high = oi // 2, lax.rem(oi, 2)
    beside = [(oi, link_to[link]) for link in range(4)]
    rows_beside = [
        (lax.rem(y_index + 1, 4) * 2 + z_high, oj),
        (lax.rem(y_index + 3, 4) * 2 + z_high, oj),
        (oi + 1 - 2 * z_high, oj),
    ]
    barrier = pltpu.get_barrier_semaphore()
    for device in beside + rows_beside:
        pl.semaphore_signal(barrier, inc=1, device_id=device, device_id_type=MESH)
    own_copy = pltpu.make_async_copy(b_hbm.at[0], ball.at[oj, pl.ds(HEAD, naux)], local_sem.at[0])
    own_copy.start()

    lane = lax.broadcasted_iota(jnp.int32, (1, dom), 1)
    occupied = occ_ref[...].astype(jnp.float32)
    own_v = [pao_ref[pl.ds(dom_ref[0, k], 1), :] - occupied for k in range(blocks)]
    rest = jnp.concatenate(own_v, axis=1)
    head = []
    for _ in range(3):
        head.append(rest.astype(jnp.bfloat16).astype(jnp.float32))
        rest = rest - head[-1]
    listed = jnp.zeros((1, dom), jnp.float32)
    for s in range(pair_ref.shape[1]):
        listed = listed + jnp.where(lane == pair_ref[0, s], 1.0, 0.0)
    head += [listed, jnp.zeros((HEAD - 4, dom), jnp.float32)]
    ball[oj, 0:HEAD, :] = jnp.concatenate(head, axis=0).astype(jnp.bfloat16)
    own_copy.wait()

    pl.semaphore_wait(barrier, len(beside + rows_beside))

    def tell(stage):
        for device in rows_beside:
            pl.semaphore_signal(known.at[stage], inc=1, device_id=device, device_id_type=MESH)

    def hear(stage):
        pl.semaphore_wait(known.at[stage], len(rows_beside))

    counts = [0, 0, 0, 0]
    started = []

    def piece(slot, k):
        if k == 0:
            return ball.at[slot, pl.ds(0, HEAD + piece_rows)]
        return ball.at[slot, pl.ds(HEAD + k * piece_rows, piece_rows)]

    def send(slot, k, link):
        copy = pltpu.make_async_remote_copy(
            src_ref=piece(slot, k),
            dst_ref=piece(slot, k),
            send_sem=link_send.at[link, counts[link]],
            recv_sem=piece_recv.at[slot, k],
            device_id=(oi, link_to[link]),
            device_id_type=MESH,
        )
        counts[link] += 1
        copy.start()
        started.append(copy)

    def wait_piece(slot, k):
        pltpu.make_async_remote_copy(
            src_ref=piece(slot, k),
            dst_ref=piece(slot, k),
            send_sem=link_send.at[0, 0],
            recv_sem=piece_recv.at[slot, k],
            device_id=(oi, sibling),
            device_id_type=MESH,
        ).wait_recv()

    for k in range(3):
        for link in (PLUS, MINUS, ZED, SIBLING):
            send(oj, k, link)

    for k in range(blocks):
        vcol[k * 128:(k + 1) * 128, :] = jnp.transpose(jnp.broadcast_to(own_v[k], (128, 128)))
    for k in range(3):
        bt[:, k * piece_rows:(k + 1) * piece_rows] = jnp.transpose(
            ball[oj, HEAD + k * piece_rows:HEAD + (k + 1) * piece_rows, :]
        )

    def block(slot, start=0, size=naux):
        return ball[slot, pl.ds(pl.multiple_of(HEAD + start, HEAD), size), :]

    def amplitudes(partner, side):
        own_head = ball[oj, 0:HEAD, :].astype(jnp.float32)
        its_head = ball[partner, 0:HEAD, :].astype(jnp.float32)
        energies = its_head[0:1] + its_head[1:2] + its_head[2:3]
        weight = jnp.sum(
            jnp.where(lane == partner, own_head[3:4], 0.0) + jnp.where(lane == oj, its_head[3:4], 0.0),
            axis=1, keepdims=True,
        )
        overlap = jnp.dot(bt[...], block(partner), preferred_element_type=jnp.float32)
        column = vcol[...]
        denominator = jnp.concatenate(
            [column + energies[:, k * 128:(k + 1) * 128] for k in range(blocks)], axis=1
        )
        mcat[:, pl.ds(pl.multiple_of(side * dom, dom), dom)] = (
            overlap * (-weight) / denominator
        ).astype(jnp.bfloat16)

    half_rows = naux // 2

    def pick(i, offsets):
        chip = chip_at(*offsets[0])
        for n, offset in enumerate(offsets[1:]):
            chip = jnp.where(i == n + 1, chip_at(*offset), chip)
        return chip

    def update(chip, start=0, size=naux):
        return (
            dot_nt(block(chip * CORES, start, size), mcat[:, :dom])
            + dot_nt(block(chip * CORES + 1, start, size), mcat[:, dom:])
        )

    def process(chip, first=False):
        for side in range(CORES):
            amplitudes(chip * CORES + side, side)

        if first:
            gsum[...] = update(chip)
        else:
            gsum[...] += update(chip)

    def process_group(offsets):
        if len(offsets) == 1:
            process(chip_at(*offsets[0]))
            return

        def step(i, carry):
            process(pick(i, offsets))
            return carry

        lax.fori_loop(0, len(offsets), step, 0)

    def arrive(dx, dz, k):
        wait_piece(place(dx, dz), k)
        send(place(dx, dz), k, SIBLING)

    def arrived_at_sibling(dx, dz):
        other = chip_at(dx, dz) * CORES + 1 - core
        for k in range(3):
            wait_piece(other, k)

    arrived_at_sibling(0, 0)
    process(chip_at(0, 0), first=True)

    for dx, dz in ((3, 0), (1, 0), (0, 1)):
        arrive(dx, dz, 0)
    send(place(3, 0), 0, PLUS)
    send(place(3, 0), 0, ZED)
    send(place(1, 0), 0, ZED)
    for dx, dz in ((3, 0), (1, 0), (0, 1)):
        arrive(dx, dz, 1)
    send(place(0, 1), 1, PLUS)
    send(place(1, 0), 1, MINUS)
    send(place(1, 0), 1, ZED)
    for dx, dz in ((3, 0), (1, 0), (0, 1)):
        arrive(dx, dz, 2)
    send(place(0, 1), 2, PLUS)
    send(place(1, 0), 2, MINUS)
    send(place(0, 1), 2, MINUS)
    near = ((3, 0), (1, 0), (0, 1))
    for offset in near:
        arrived_at_sibling(*offset)
    process_group(near)

    arrive(2, 0, 0)
    send(place(2, 0), 0, ZED)
    arrive(2, 0, 1)
    arrive(3, 1, 0)
    arrive(3, 1, 1)
    send(place(3, 1), 1, PLUS)
    arrive(2, 0, 2)
    arrive(1, 1, 0)
    arrived_at_sibling(2, 0)
    process_group(((2, 0),))
    arrive(1, 1, 2)
    send(place(1, 1), 2, MINUS)
    arrive(3, 1, 2)
    arrive(1, 1, 1)
    diagonal = ((3, 1), (1, 1))
    for offset in diagonal:
        arrived_at_sibling(*offset)
    process_group(diagonal)
    last = chip_at(2, 1)
    for k in range(3):
        arrive(2, 1, k)

    amplitudes(last * CORES + core, core)
    arrived_at_sibling(2, 1)
    tell(0)
    amplitudes(last * CORES + 1 - core, 1 - core)

    def slice_rows_of(position):
        return pl.ds(pl.multiple_of(slice_of(position) * slice_rows, slice_rows), slice_rows)

    def gamma_copy(target, source, where):
        return pltpu.make_async_remote_copy(
            src_ref=gout.at[slice_rows_of(target)],
            dst_ref=gall.at[source],
            send_sem=gam_send.at[target],
            recv_sem=gam_recv.at[source],
            device_id=(oi, where),
            device_id_type=MESH,
        )

    own_slice = pltpu.make_async_copy(gout.at[slice_rows_of(oj)], gall.at[oj], local_sem.at[1])

    def out_copy(i):
        rows = pl.ds(pl.multiple_of(i * half_rows, half_rows), half_rows)
        return pltpu.make_async_copy(gout.at[rows], gamma_out.at[0, rows], local_sem.at[3 + i])

    ring = ((2, 1), (2, 0), (1, 1), (3, 1), (1, 0), (3, 0), (0, 1), (0, 0))

    def finish(i, carry):
        part = lax.rem(x // 2 + 1 + i, 2)
        rows = pl.ds(pl.multiple_of(part * half_rows, half_rows), half_rows)
        term = update(last, part * half_rows, half_rows)
        gout[rows, :] = (gsum[rows, :] + term).astype(jnp.bfloat16)

        def leave(n, inner):
            chip = pick(n, ring)
            for k in range(CORES):
                target = chip * CORES + lax.rem(core + k, CORES)
                here = lax.rem(chip, CHIPS_X) // 2 == part

                @pl.when(jnp.logical_and(here, target != oj))
                def _():
                    gamma_copy(target, oj, target).start()

                @pl.when(jnp.logical_and(here, target == oj))
                def _():
                    own_slice.start()
            return inner

        lax.fori_loop(0, ROW // CORES, leave, 0)
        out_copy(part).start()
        return carry

    lax.fori_loop(0, 2, finish, 0)
    hear(0)
    tell(1)
    for copy in started:
        copy.wait_send()

    dacc[...] = jnp.zeros_like(dacc)

    def density(i, carry):
        for n in range(2):
            chip = pick(2 * i + n, ring)
            for k in range(CORES):
                source = chip * CORES + k

                @pl.when(source == oj)
                def _():
                    own_slice.wait()

                @pl.when(source != oj)
                def _():
                    gamma_copy(source, source, source).wait_recv()

        terms = [
            dot_nt(gall[pick(2 * i + n, ring) * CORES + k], block(pick(2 * i + n, ring) * CORES + k))
            for n in range(2) for k in range(CORES)
        ]
        dacc[...] += (terms[0] + terms[1]) + (terms[2] + terms[3])
        return carry

    lax.fori_loop(0, 1, density, 0)
    hear(1)
    tell(2)
    lax.fori_loop(1, ROW // CORES // 2, density, 0)
    hear(2)
    groups = 4
    lanes = naux // groups
    for t in range(n_oi):
        rows = dacc[t * strip:(t + 1) * strip, :]
        dpart[t] = jnp.concatenate(
            [rows[:, g * lanes:(g + 1) * lanes] for g in range(groups)], axis=0
        ).astype(jnp.bfloat16)

    def den_copy(t, row, where):
        return pltpu.make_async_remote_copy(
            src_ref=dpart.at[t],
            dst_ref=dall.at[row],
            send_sem=den_send.at[t],
            recv_sem=den_recv.at[row],
            device_id=where,
            device_id_type=MESH,
        )

    own_strip = me - first_owner

    def keep_copy():
        return pltpu.make_async_copy(dpart.at[jnp.clip(own_strip, 0, n_oi - 1)], dall.at[oi], local_sem.at[2])

    for t in range(n_oi):
        @pl.when(first_owner + t != me)
        def _():
            den_copy(t, oi, owner(t)).start()

    @pl.when(self_owner)
    def _():
        keep_copy().start()

    for t in range(2):
        out_copy(t).wait()

    def drain(target, carry):
        @pl.when(target != oj)
        def _():
            gamma_copy(target, oj, target).wait_send()
        return carry

    lax.fori_loop(0, ROW, drain, 0)
    @pl.when(self_owner)
    def _():
        keep_copy().wait()

    for row in range(n_oi):
        @pl.when(jnp.logical_or(oi != row, oj != my_slice))
        def _():
            den_copy(0, row, (row, my_slice)).wait_recv()
    total = dall[0].astype(jnp.float32)
    for row in range(1, n_oi):
        total = total + dall[row].astype(jnp.float32)
    total = total * (1.0 / (n_oi * ROW))
    dens_out[...] = jnp.concatenate(
        [total[g * strip:(g + 1) * strip] for g in range(groups)], axis=1
    ).astype(jnp.bfloat16)

    for t in range(n_oi):
        @pl.when(first_owner + t != me)
        def _():
            den_copy(t, oi, owner(t)).wait_send()


def body(n_oi, b_tensor, occ_energy, dom_blocks, pair_cols, pao_energy):
    naux, dom = b_tensor.shape[1], b_tensor.shape[2]
    slice_rows = naux // ROW
    strip = slice_rows // n_oi
    vmem = pl.BlockSpec(memory_space=pltpu.VMEM)
    smem = pl.BlockSpec(memory_space=pltpu.SMEM)
    hbm = pl.BlockSpec(memory_space=pl.ANY)
    dma = pltpu.SemaphoreType.DMA
    return pl.pallas_call(
        functools.partial(kernel, n_oi),
        out_shape=(
            jax.ShapeDtypeStruct((1, naux, dom), jnp.bfloat16),
            jax.ShapeDtypeStruct((strip, naux), jnp.bfloat16),
        ),
        in_specs=[hbm, vmem, smem, smem, vmem],
        out_specs=(hbm, vmem),
        scratch_shapes=[
            pltpu.VMEM((ROW, HEAD + naux, dom), jnp.bfloat16),
            pltpu.VMEM((dom, naux), jnp.bfloat16),
            pltpu.VMEM((naux, dom), jnp.float32),
            pltpu.VMEM((naux, dom), jnp.bfloat16),
            pltpu.VMEM((ROW, slice_rows, dom), jnp.bfloat16),
            pltpu.VMEM((dom, CORES * dom), jnp.bfloat16),
            pltpu.VMEM((slice_rows, naux), jnp.float32),
            pltpu.VMEM((n_oi, 4 * strip, naux // 4), jnp.bfloat16),
            pltpu.VMEM((n_oi, 4 * strip, naux // 4), jnp.bfloat16),
            pltpu.VMEM((dom, 128), jnp.float32),
            dma((4, 24)),
            dma((ROW, 3)),
            dma((ROW,)),
            dma((ROW,)),
            dma((n_oi,)),
            dma((n_oi,)),
            dma((5,)),
            pltpu.SemaphoreType.REGULAR((3,)),
        ],
        compiler_params=pltpu.CompilerParams(
            collective_id=0, has_side_effects=True, vmem_limit_bytes=56 * 2**20
        ),
        cost_estimate=pl.CostEstimate(
            flops=2 * naux * dom * dom * 32, bytes_accessed=4 * naux * dom, transcendentals=0
        ),
    )(b_tensor, occ_energy.reshape(1, 1), dom_blocks, pair_cols, pao_energy)


def solution(mesh):
    in_specs = (
        P(("oi", "oj"), None, None),
        P(("oi", "oj")),
        P(("oi", "oj"), None),
        P(("oi", "oj"), None),
        P(),
    )
    out_specs = (P(("oi", "oj"), None, None), P(("oi", "oj"), None))
    return jax.shard_map(
        functools.partial(body, mesh.shape["oi"]),
        mesh=mesh, in_specs=in_specs, out_specs=out_specs, check_vma=False,
    )
```

```python
import functools

import jax
import jax.numpy as jnp
from jax import lax
from jax.experimental import pallas as pl
from jax.experimental.pallas import tpu as pltpu
from jax.sharding import PartitionSpec as P

MESH = pl.DeviceIdType.MESH
PLUS, MINUS, ZED, SIBLING = range(4)
CHIPS_X, CHIPS_Z, CORES = 4, 2, 2
ROW = CHIPS_X * CHIPS_Z * CORES
HEAD = 16


def dot_nt(lhs, rhs):
    return lax.dot_general(lhs, rhs, (((1,), (1,)), ((), ())), preferred_element_type=jnp.float32)


def kernel(
    n_oi, b_hbm, occ_ref, dom_hbm, pair_hbm, pao_hbm, gamma_out, dens_out,
    dom_ref, pair_ref, pao_ref, ball, bt, gsum, gout, gall, mcat, dacc, dpart, dall, vcol,
    link_send, piece_recv, gam_send, gam_recv, den_send, den_recv, local_sem, known,
):
    naux, dom = b_hbm.shape[1], b_hbm.shape[2]
    blocks = dom // 128
    piece_rows = naux // 3
    slice_rows = naux // ROW
    strip = slice_rows // n_oi
    oi, oj = lax.axis_index("oi"), lax.axis_index("oj")
    core, x, z = lax.rem(oj, 2), lax.rem(oj // 2, CHIPS_X), oj // (CHIPS_X * CORES)

    def chip_at(dx, dz):
        return lax.rem(z + dz, CHIPS_Z) * CHIPS_X + lax.rem(x + dx, CHIPS_X)

    def place(dx, dz):
        return chip_at(dx, dz) * CORES + core

    sibling = oj + 1 - 2 * core
    link_to = {PLUS: place(1, 0), MINUS: place(3, 0), ZED: place(0, 1), SIBLING: sibling}

    def slice_of(position):
        return (
            lax.rem(position // CORES, CHIPS_X) * (CORES * CHIPS_Z)
            + lax.rem(position, CORES) * CHIPS_Z
            + position // (CHIPS_X * CORES)
        )

    def position_of(part):
        return (
            lax.rem(part, CHIPS_Z) * CHIPS_X + part // (CORES * CHIPS_Z)
        ) * CORES + lax.rem(part // CHIPS_Z, CORES)

    me = oi * ROW + oj
    first_owner = slice_of(oj) * n_oi
    my_slice = position_of(me // n_oi)
    self_owner = jnp.logical_and(first_owner <= me, me < first_owner + n_oi)

    def owner(t):
        flat = first_owner + t
        return flat // ROW, lax.rem(flat, ROW)

    y_index, z_high = oi // 2, lax.rem(oi, 2)
    beside = [(oi, link_to[link]) for link in range(4)]
    rows_beside = [
        (lax.rem(y_index + 1, 4) * 2 + z_high, oj),
        (lax.rem(y_index + 3, 4) * 2 + z_high, oj),
        (oi + 1 - 2 * z_high, oj),
    ]
    barrier = pltpu.get_barrier_semaphore()
    for device in beside + rows_beside:
        pl.semaphore_signal(barrier, inc=1, device_id=device, device_id_type=MESH)
    own_copy = pltpu.make_async_copy(b_hbm.at[0], ball.at[oj, pl.ds(HEAD, naux)], local_sem.at[0])
    fetches = [
        pltpu.make_async_copy(source, target, local_sem.at[5 + n])
        for n, (source, target) in enumerate(((dom_hbm, dom_ref), (pair_hbm, pair_ref), (pao_hbm, pao_ref)))
    ]
    for fetch in fetches:
        fetch.start()
    own_copy.start()
    for fetch in fetches:
        fetch.wait()

    lane = lax.broadcasted_iota(jnp.int32, (1, dom), 1)
    occupied = occ_ref[...].astype(jnp.float32)
    own_v = [pao_ref[pl.ds(dom_ref[0, k], 1), :] - occupied for k in range(blocks)]
    rest = jnp.concatenate(own_v, axis=1)
    head = []
    for _ in range(3):
        head.append(rest.astype(jnp.bfloat16).astype(jnp.float32))
        rest = rest - head[-1]
    listed = jnp.zeros((1, dom), jnp.float32)
    for s in range(pair_ref.shape[1]):
        listed = listed + jnp.where(lane == pair_ref[0, s], 1.0, 0.0)
    head += [listed, jnp.zeros((HEAD - 4, dom), jnp.float32)]
    ball[oj, 0:HEAD, :] = jnp.concatenate(head, axis=0).astype(jnp.bfloat16)
    own_copy.wait()

    pl.semaphore_wait(barrier, len(beside + rows_beside))

    def tell(stage):
        for device in rows_beside:
            pl.semaphore_signal(known.at[stage], inc=1, device_id=device, device_id_type=MESH)

    def hear(stage):
        pl.semaphore_wait(known.at[stage], len(rows_beside))

    counts = [0, 0, 0, 0]
    started = []

    def piece(slot, k):
        if k == 0:
            return ball.at[slot, pl.ds(0, HEAD + piece_rows)]
        return ball.at[slot, pl.ds(HEAD + k * piece_rows, piece_rows)]

    def send(slot, k, link):
        copy = pltpu.make_async_remote_copy(
            src_ref=piece(slot, k),
            dst_ref=piece(slot, k),
            send_sem=link_send.at[link, counts[link]],
            recv_sem=piece_recv.at[slot, k],
            device_id=(oi, link_to[link]),
            device_id_type=MESH,
        )
        counts[link] += 1
        copy.start()
        started.append(copy)

    def wait_piece(slot, k):
        pltpu.make_async_remote_copy(
            src_ref=piece(slot, k),
            dst_ref=piece(slot, k),
            send_sem=link_send.at[0, 0],
            recv_sem=piece_recv.at[slot, k],
            device_id=(oi, sibling),
            device_id_type=MESH,
        ).wait_recv()

    for k in range(3):
        for link in (PLUS, MINUS, ZED, SIBLING):
            send(oj, k, link)

    for k in range(blocks):
        vcol[k * 128:(k + 1) * 128, :] = jnp.transpose(jnp.broadcast_to(own_v[k], (128, 128)))
    for k in range(3):
        bt[:, k * piece_rows:(k + 1) * piece_rows] = jnp.transpose(
            ball[oj, HEAD + k * piece_rows:HEAD + (k + 1) * piece_rows, :]
        )

    def block(slot, start=0, size=naux):
        return ball[slot, pl.ds(pl.multiple_of(HEAD + start, HEAD), size), :]

    def amplitudes(partner, side):
        own_head = ball[oj, 0:HEAD, :].astype(jnp.float32)
        its_head = ball[partner, 0:HEAD, :].astype(jnp.float32)
        energies = its_head[0:1] + its_head[1:2] + its_head[2:3]
        weight = jnp.sum(
            jnp.where(lane == partner, own_head[3:4], 0.0) + jnp.where(lane == oj, its_head[3:4], 0.0),
            axis=1, keepdims=True,
        )
        overlap = jnp.dot(bt[...], block(partner), preferred_element_type=jnp.float32)
        column = vcol[...]
        denominator = jnp.concatenate(
            [column + energies[:, k * 128:(k + 1) * 128] for k in range(blocks)], axis=1
        )
        mcat[:, pl.ds(pl.multiple_of(side * dom, dom), dom)] = (
            overlap * (-weight) / denominator
        ).astype(jnp.bfloat16)

    half_rows = naux // 2

    def pick(i, offsets):
        chip = chip_at(*offsets[0])
        for n, offset in enumerate(offsets[1:]):
            chip = jnp.where(i == n + 1, chip_at(*offset), chip)
        return chip

    def update(chip, start=0, size=naux):
        return (
            dot_nt(block(chip * CORES, start, size), mcat[:, :dom])
            + dot_nt(block(chip * CORES + 1, start, size), mcat[:, dom:])
        )

    def process(chip, first=False):
        for side in range(CORES):
            amplitudes(chip * CORES + side, side)

        if first:
            gsum[...] = update(chip)
        else:
            gsum[...] += update(chip)

    def process_group(offsets):
        if len(offsets) == 1:
            process(chip_at(*offsets[0]))
            return

        def step(i, carry):
            process(pick(i, offsets))
            return carry

        lax.fori_loop(0, len(offsets), step, 0)

    def arrive(dx, dz, k):
        wait_piece(place(dx, dz), k)
        send(place(dx, dz), k, SIBLING)

    def arrived_at_sibling(dx, dz):
        other = chip_at(dx, dz) * CORES + 1 - core
        for k in range(3):
            wait_piece(other, k)

    arrived_at_sibling(0, 0)
    process(chip_at(0, 0), first=True)

    for dx, dz in ((3, 0), (1, 0), (0, 1)):
        arrive(dx, dz, 0)
    send(place(3, 0), 0, PLUS)
    send(place(3, 0), 0, ZED)
    send(place(1, 0), 0, ZED)
    for dx, dz in ((3, 0), (1, 0), (0, 1)):
        arrive(dx, dz, 1)
    send(place(0, 1), 1, PLUS)
    send(place(1, 0), 1, MINUS)
    send(place(1, 0), 1, ZED)
    for dx, dz in ((3, 0), (1, 0), (0, 1)):
        arrive(dx, dz, 2)
    send(place(0, 1), 2, PLUS)
    send(place(1, 0), 2, MINUS)
    send(place(0, 1), 2, MINUS)
    near = ((3, 0), (1, 0), (0, 1))
    for offset in near:
        arrived_at_sibling(*offset)
    process_group(near)

    arrive(2, 0, 0)
    send(place(2, 0), 0, ZED)
    arrive(2, 0, 1)
    arrive(3, 1, 0)
    arrive(3, 1, 1)
    send(place(3, 1), 1, PLUS)
    arrive(2, 0, 2)
    arrive(1, 1, 0)
    arrived_at_sibling(2, 0)
    process_group(((2, 0),))
    arrive(1, 1, 2)
    send(place(1, 1), 2, MINUS)
    arrive(3, 1, 2)
    arrive(1, 1, 1)
    diagonal = ((3, 1), (1, 1))
    for offset in diagonal:
        arrived_at_sibling(*offset)
    process_group(diagonal)
    last = chip_at(2, 1)
    for k in range(3):
        arrive(2, 1, k)

    amplitudes(last * CORES + core, core)
    arrived_at_sibling(2, 1)
    tell(0)
    amplitudes(last * CORES + 1 - core, 1 - core)

    def slice_rows_of(position):
        return pl.ds(pl.multiple_of(slice_of(position) * slice_rows, slice_rows), slice_rows)

    def gamma_copy(target, source, where):
        return pltpu.make_async_remote_copy(
            src_ref=gout.at[slice_rows_of(target)],
            dst_ref=gall.at[source],
            send_sem=gam_send.at[target],
            recv_sem=gam_recv.at[source],
            device_id=(oi, where),
            device_id_type=MESH,
        )

    own_slice = pltpu.make_async_copy(gout.at[slice_rows_of(oj)], gall.at[oj], local_sem.at[1])

    def out_copy(i):
        rows = pl.ds(pl.multiple_of(i * half_rows, half_rows), half_rows)
        return pltpu.make_async_copy(gout.at[rows], gamma_out.at[0, rows], local_sem.at[3 + i])

    ring = ((2, 1), (2, 0), (1, 1), (3, 1), (1, 0), (3, 0), (0, 1), (0, 0))

    def finish(i, carry):
        part = lax.rem(x // 2 + 1 + i, 2)
        rows = pl.ds(pl.multiple_of(part * half_rows, half_rows), half_rows)
        term = update(last, part * half_rows, half_rows)
        gout[rows, :] = (gsum[rows, :] + term).astype(jnp.bfloat16)

        def leave(n, inner):
            chip = pick(n, ring)
            for k in range(CORES):
                target = chip * CORES + lax.rem(core + k, CORES)
                here = lax.rem(chip, CHIPS_X) // 2 == part

                @pl.when(jnp.logical_and(here, target != oj))
                def _():
                    gamma_copy(target, oj, target).start()

                @pl.when(jnp.logical_and(here, target == oj))
                def _():
                    own_slice.start()
            return inner

        lax.fori_loop(0, ROW // CORES, leave, 0)
        out_copy(part).start()
        return carry

    lax.fori_loop(0, 2, finish, 0)
    hear(0)
    tell(1)
    for copy in started:
        copy.wait_send()

    dacc[...] = jnp.zeros_like(dacc)

    def density(i, carry):
        for n in range(2):
            chip = pick(2 * i + n, ring)
            for k in range(CORES):
                source = chip * CORES + k

                @pl.when(source == oj)
                def _():
                    own_slice.wait()

                @pl.when(source != oj)
                def _():
                    gamma_copy(source, source, source).wait_recv()

        terms = [
            dot_nt(gall[pick(2 * i + n, ring) * CORES + k], block(pick(2 * i + n, ring) * CORES + k))
            for n in range(2) for k in range(CORES)
        ]
        dacc[...] += (terms[0] + terms[1]) + (terms[2] + terms[3])
        return carry

    lax.fori_loop(0, 1, density, 0)
    hear(1)
    tell(2)
    lax.fori_loop(1, ROW // CORES // 2, density, 0)
    hear(2)
    groups = 4
    lanes = naux // groups
    for t in range(n_oi):
        rows = dacc[t * strip:(t + 1) * strip, :]
        dpart[t] = jnp.concatenate(
            [rows[:, g * lanes:(g + 1) * lanes] for g in range(groups)], axis=0
        ).astype(jnp.bfloat16)

    def den_copy(t, row, where):
        return pltpu.make_async_remote_copy(
            src_ref=dpart.at[t],
            dst_ref=dall.at[row],
            send_sem=den_send.at[t],
            recv_sem=den_recv.at[row],
            device_id=where,
            device_id_type=MESH,
        )

    own_strip = me - first_owner

    def keep_copy():
        return pltpu.make_async_copy(dpart.at[jnp.clip(own_strip, 0, n_oi - 1)], dall.at[oi], local_sem.at[2])

    for t in range(n_oi):
        @pl.when(first_owner + t != me)
        def _():
            den_copy(t, oi, owner(t)).start()

    @pl.when(self_owner)
    def _():
        keep_copy().start()

    for t in range(2):
        out_copy(t).wait()

    def drain(target, carry):
        @pl.when(target != oj)
        def _():
            gamma_copy(target, oj, target).wait_send()
        return carry

    lax.fori_loop(0, ROW, drain, 0)
    @pl.when(self_owner)
    def _():
        keep_copy().wait()

    for row in range(n_oi):
        @pl.when(jnp.logical_or(oi != row, oj != my_slice))
        def _():
            den_copy(0, row, (row, my_slice)).wait_recv()
    total = dall[0].astype(jnp.float32)
    for row in range(1, n_oi):
        total = total + dall[row].astype(jnp.float32)
    total = total * (1.0 / (n_oi * ROW))
    dens_out[...] = jnp.concatenate(
        [total[g * strip:(g + 1) * strip] for g in range(groups)], axis=1
    ).astype(jnp.bfloat16)

    for t in range(n_oi):
        @pl.when(first_owner + t != me)
        def _():
            den_copy(t, oi, owner(t)).wait_send()


def body(n_oi, b_tensor, occ_energy, dom_blocks, pair_cols, pao_energy):
    naux, dom = b_tensor.shape[1], b_tensor.shape[2]
    slice_rows = naux // ROW
    strip = slice_rows // n_oi
    vmem = pl.BlockSpec(memory_space=pltpu.VMEM)
    hbm = pl.BlockSpec(memory_space=pl.ANY)
    dma = pltpu.SemaphoreType.DMA
    return pl.pallas_call(
        functools.partial(kernel, n_oi),
        out_shape=(
            jax.ShapeDtypeStruct((1, naux, dom), jnp.bfloat16),
            jax.ShapeDtypeStruct((strip, naux), jnp.bfloat16),
        ),
        in_specs=[hbm, vmem, hbm, hbm, hbm],
        out_specs=(hbm, vmem),
        scratch_shapes=[
            pltpu.SMEM(dom_blocks.shape, jnp.int32),
            pltpu.SMEM(pair_cols.shape, jnp.int32),
            pltpu.VMEM(pao_energy.shape, jnp.float32),
            pltpu.VMEM((ROW, HEAD + naux, dom), jnp.bfloat16),
            pltpu.VMEM((dom, naux), jnp.bfloat16),
            pltpu.VMEM((naux, dom), jnp.float32),
            pltpu.VMEM((naux, dom), jnp.bfloat16),
            pltpu.VMEM((ROW, slice_rows, dom), jnp.bfloat16),
            pltpu.VMEM((dom, CORES * dom), jnp.bfloat16),
            pltpu.VMEM((slice_rows, naux), jnp.float32),
            pltpu.VMEM((n_oi, 4 * strip, naux // 4), jnp.bfloat16),
            pltpu.VMEM((n_oi, 4 * strip, naux // 4), jnp.bfloat16),
            pltpu.VMEM((dom, 128), jnp.float32),
            dma((4, 24)),
            dma((ROW, 3)),
            dma((ROW,)),
            dma((ROW,)),
            dma((n_oi,)),
            dma((n_oi,)),
            dma((8,)),
            pltpu.SemaphoreType.REGULAR((3,)),
        ],
        compiler_params=pltpu.CompilerParams(
            collective_id=0, has_side_effects=True, vmem_limit_bytes=52 * 2**20
        ),
        cost_estimate=pl.CostEstimate(
            flops=2 * naux * dom * dom * 32, bytes_accessed=4 * naux * dom, transcendentals=0
        ),
    )(b_tensor, occ_energy.reshape(1, 1), dom_blocks, pair_cols, pao_energy)


def solution(mesh):
    in_specs = (
        P(("oi", "oj"), None, None),
        P(("oi", "oj")),
        P(("oi", "oj"), None),
        P(("oi", "oj"), None),
        P(),
    )
    out_specs = (P(("oi", "oj"), None, None), P(("oi", "oj"), None))
    return jax.shard_map(
        functools.partial(body, mesh.shape["oi"]),
        mesh=mesh, in_specs=in_specs, out_specs=out_specs, check_vma=False,
    )
```

```python
import functools

import jax
import jax.numpy as jnp
from jax import lax
from jax.experimental import pallas as pl
from jax.experimental.pallas import tpu as pltpu
from jax.sharding import PartitionSpec as P

MESH = pl.DeviceIdType.MESH
PLUS, MINUS, ZED, SIBLING = range(4)
CHIPS_X, CHIPS_Z, CORES = 4, 2, 2
ROW = CHIPS_X * CHIPS_Z * CORES
HEAD = 16


def dot_nt(lhs, rhs):
    return lax.dot_general(lhs, rhs, (((1,), (1,)), ((), ())), preferred_element_type=jnp.float32)


def kernel(
    n_oi, b_hbm, occ_ref, dom_hbm, pair_hbm, pao_hbm, gamma_out, dens_out,
    dom_ref, pair_ref, pao_ref, ball, bt, gsum, gout, gall, mcat, dacc, dpart, dall, vcol,
    link_send, piece_recv, gam_send, gam_recv, den_send, den_recv, local_sem, known,
):
    naux, dom = b_hbm.shape[1], b_hbm.shape[2]
    blocks = dom // 128
    piece_rows = naux // 3
    slice_rows = naux // ROW
    strip = slice_rows // n_oi
    oi, oj = lax.axis_index("oi"), lax.axis_index("oj")
    core, x, z = lax.rem(oj, 2), lax.rem(oj // 2, CHIPS_X), oj // (CHIPS_X * CORES)

    def chip_at(dx, dz):
        return lax.rem(z + dz, CHIPS_Z) * CHIPS_X + lax.rem(x + dx, CHIPS_X)

    def place(dx, dz):
        return chip_at(dx, dz) * CORES + core

    sibling = oj + 1 - 2 * core
    link_to = {PLUS: place(1, 0), MINUS: place(3, 0), ZED: place(0, 1), SIBLING: sibling}

    def slice_of(position):
        return (
            lax.rem(position // CORES, CHIPS_X) * (CORES * CHIPS_Z)
            + lax.rem(position, CORES) * CHIPS_Z
            + position // (CHIPS_X * CORES)
        )

    def position_of(part):
        return (
            lax.rem(part, CHIPS_Z) * CHIPS_X + part // (CORES * CHIPS_Z)
        ) * CORES + lax.rem(part // CHIPS_Z, CORES)

    me = oi * ROW + oj
    first_owner = slice_of(oj) * n_oi
    my_slice = position_of(me // n_oi)
    self_owner = jnp.logical_and(first_owner <= me, me < first_owner + n_oi)

    def owner(t):
        flat = first_owner + t
        return flat // ROW, lax.rem(flat, ROW)

    y_index, z_high = oi // 2, lax.rem(oi, 2)
    beside = [(oi, link_to[link]) for link in range(4)]
    rows_beside = [
        (lax.rem(y_index + 1, 4) * 2 + z_high, oj),
        (lax.rem(y_index + 3, 4) * 2 + z_high, oj),
        (oi + 1 - 2 * z_high, oj),
    ]
    barrier = pltpu.get_barrier_semaphore()
    for device in beside + rows_beside:
        pl.semaphore_signal(barrier, inc=1, device_id=device, device_id_type=MESH)
    own_copy = pltpu.make_async_copy(b_hbm.at[0], ball.at[oj, pl.ds(HEAD, naux)], local_sem.at[0])
    fetches = [
        pltpu.make_async_copy(source, target, local_sem.at[5 + n])
        for n, (source, target) in enumerate(((dom_hbm, dom_ref), (pair_hbm, pair_ref), (pao_hbm, pao_ref)))
    ]
    for fetch in fetches:
        fetch.start()
    own_copy.start()
    for fetch in fetches:
        fetch.wait()

    lane = lax.broadcasted_iota(jnp.int32, (1, dom), 1)
    occupied = occ_ref[...].astype(jnp.float32)
    own_v = [pao_ref[pl.ds(dom_ref[0, k], 1), :] - occupied for k in range(blocks)]
    rest = jnp.concatenate(own_v, axis=1)
    head = []
    for _ in range(3):
        head.append(rest.astype(jnp.bfloat16).astype(jnp.float32))
        rest = rest - head[-1]
    listed = jnp.zeros((1, dom), jnp.float32)
    for s in range(pair_ref.shape[1]):
        listed = listed + jnp.where(lane == pair_ref[0, s], 1.0, 0.0)
    head += [listed, jnp.zeros((HEAD - 4, dom), jnp.float32)]
    ball[oj, 0:HEAD, :] = jnp.concatenate(head, axis=0).astype(jnp.bfloat16)
    own_copy.wait()

    pl.semaphore_wait(barrier, len(beside + rows_beside))

    def tell(stage):
        for device in rows_beside:
            pl.semaphore_signal(known.at[stage], inc=1, device_id=device, device_id_type=MESH)

    def hear(stage):
        pl.semaphore_wait(known.at[stage], len(rows_beside))

    counts = [0, 0, 0, 0]
    started = []

    def piece(slot, k):
        if k == 0:
            return ball.at[slot, pl.ds(0, HEAD + piece_rows)]
        return ball.at[slot, pl.ds(HEAD + k * piece_rows, piece_rows)]

    def send(slot, k, link):
        copy = pltpu.make_async_remote_copy(
            src_ref=piece(slot, k),
            dst_ref=piece(slot, k),
            send_sem=link_send.at[link, counts[link]],
            recv_sem=piece_recv.at[slot, k],
            device_id=(oi, link_to[link]),
            device_id_type=MESH,
        )
        counts[link] += 1
        copy.start()
        started.append(copy)

    def wait_piece(slot, k):
        pltpu.make_async_remote_copy(
            src_ref=piece(slot, k),
            dst_ref=piece(slot, k),
            send_sem=link_send.at[0, 0],
            recv_sem=piece_recv.at[slot, k],
            device_id=(oi, sibling),
            device_id_type=MESH,
        ).wait_recv()

    for k in range(3):
        for link in (PLUS, MINUS, ZED, SIBLING):
            send(oj, k, link)

    for k in range(blocks):
        vcol[k * 128:(k + 1) * 128, :] = jnp.transpose(jnp.broadcast_to(own_v[k], (128, 128)))
    for k in range(3):
        bt[:, k * piece_rows:(k + 1) * piece_rows] = jnp.transpose(
            ball[oj, HEAD + k * piece_rows:HEAD + (k + 1) * piece_rows, :]
        )

    def block(slot, start=0, size=naux):
        return ball[slot, pl.ds(pl.multiple_of(HEAD + start, HEAD), size), :]

    def amplitudes(partner, side):
        own_head = ball[oj, 0:HEAD, :].astype(jnp.float32)
        its_head = ball[partner, 0:HEAD, :].astype(jnp.float32)
        energies = its_head[0:1] + its_head[1:2] + its_head[2:3]
        weight = jnp.sum(
            jnp.where(lane == partner, own_head[3:4], 0.0) + jnp.where(lane == oj, its_head[3:4], 0.0),
            axis=1, keepdims=True,
        )
        overlap = jnp.dot(bt[...], block(partner), preferred_element_type=jnp.float32)
        column = vcol[...]
        denominator = jnp.concatenate(
            [column + energies[:, k * 128:(k + 1) * 128] for k in range(blocks)], axis=1
        )
        mcat[:, pl.ds(pl.multiple_of(side * dom, dom), dom)] = (
            overlap * (-weight) / denominator
        ).astype(jnp.bfloat16)

    half_rows = naux // 2

    def pick(i, offsets):
        chip = chip_at(*offsets[0])
        for n, offset in enumerate(offsets[1:]):
            chip = jnp.where(i == n + 1, chip_at(*offset), chip)
        return chip

    def update(chip, start=0, size=naux):
        return (
            dot_nt(block(chip * CORES, start, size), mcat[:, :dom])
            + dot_nt(block(chip * CORES + 1, start, size), mcat[:, dom:])
        )

    def process(chip, first=False):
        for side in range(CORES):
            amplitudes(chip * CORES + side, side)

        if first:
            gsum[...] = update(chip)
        else:
            gsum[...] += update(chip)

    def process_group(offsets):
        if len(offsets) == 1:
            process(chip_at(*offsets[0]))
            return

        def step(i, carry):
            process(pick(i, offsets))
            return carry

        lax.fori_loop(0, len(offsets), step, 0)

    def arrive(dx, dz, k):
        wait_piece(place(dx, dz), k)
        send(place(dx, dz), k, SIBLING)

    def arrived_at_sibling(dx, dz):
        other = chip_at(dx, dz) * CORES + 1 - core
        for k in range(3):
            wait_piece(other, k)

    arrived_at_sibling(0, 0)
    process(chip_at(0, 0), first=True)

    for dx, dz in ((3, 0), (1, 0), (0, 1)):
        arrive(dx, dz, 0)
    send(place(3, 0), 0, PLUS)
    send(place(3, 0), 0, ZED)
    send(place(1, 0), 0, ZED)
    for dx, dz in ((3, 0), (1, 0), (0, 1)):
        arrive(dx, dz, 1)
    send(place(0, 1), 1, PLUS)
    send(place(1, 0), 1, MINUS)
    send(place(1, 0), 1, ZED)
    for dx, dz in ((3, 0), (1, 0), (0, 1)):
        arrive(dx, dz, 2)
    send(place(0, 1), 2, PLUS)
    send(place(1, 0), 2, MINUS)
    send(place(0, 1), 2, MINUS)
    near = ((3, 0), (1, 0), (0, 1))
    for offset in near:
        arrived_at_sibling(*offset)
    process_group(near)

    arrive(2, 0, 0)
    send(place(2, 0), 0, ZED)
    arrive(2, 0, 1)
    arrive(3, 1, 0)
    arrive(3, 1, 1)
    send(place(3, 1), 1, PLUS)
    arrive(2, 0, 2)
    arrive(1, 1, 0)
    arrived_at_sibling(2, 0)
    process_group(((2, 0),))
    arrive(1, 1, 2)
    send(place(1, 1), 2, MINUS)
    arrive(3, 1, 2)
    arrive(1, 1, 1)
    diagonal = ((3, 1), (1, 1))
    for offset in diagonal:
        arrived_at_sibling(*offset)
    process_group(diagonal)
    last = chip_at(2, 1)
    for k in range(3):
        arrive(2, 1, k)

    amplitudes(last * CORES + core, core)
    arrived_at_sibling(2, 1)
    tell(0)
    amplitudes(last * CORES + 1 - core, 1 - core)

    def slice_rows_of(position):
        return pl.ds(pl.multiple_of(slice_of(position) * slice_rows, slice_rows), slice_rows)

    def gamma_copy(target, source, where):
        return pltpu.make_async_remote_copy(
            src_ref=gout.at[slice_rows_of(target)],
            dst_ref=gall.at[source],
            send_sem=gam_send.at[target],
            recv_sem=gam_recv.at[source],
            device_id=(oi, where),
            device_id_type=MESH,
        )

    own_slice = pltpu.make_async_copy(gout.at[slice_rows_of(oj)], gall.at[oj], local_sem.at[1])

    def out_copy(i):
        rows = pl.ds(pl.multiple_of(i * half_rows, half_rows), half_rows)
        return pltpu.make_async_copy(gout.at[rows], gamma_out.at[0, rows], local_sem.at[3 + i])

    ring = ((2, 1), (2, 0), (1, 1), (3, 1), (1, 0), (3, 0), (0, 1), (0, 0))

    def finish(i, carry):
        part = lax.rem(x // 2 + 1 + i, 2)
        rows = pl.ds(pl.multiple_of(part * half_rows, half_rows), half_rows)
        term = update(last, part * half_rows, half_rows)
        gout[rows, :] = (gsum[rows, :] + term).astype(jnp.bfloat16)

        def leave(n, inner):
            chip = pick(n, ring)
            for k in range(CORES):
                target = chip * CORES + lax.rem(core + k, CORES)
                here = lax.rem(chip, CHIPS_X) // 2 == part

                @pl.when(jnp.logical_and(here, target != oj))
                def _():
                    gamma_copy(target, oj, target).start()

                @pl.when(jnp.logical_and(here, target == oj))
                def _():
                    own_slice.start()
            return inner

        lax.fori_loop(0, ROW // CORES, leave, 0)
        out_copy(part).start()
        return carry

    lax.fori_loop(0, 2, finish, 0)
    hear(0)
    tell(1)
    for copy in started:
        copy.wait_send()

    dacc[...] = jnp.zeros_like(dacc)

    def slices_in(i):
        for n in range(2):
            chip = pick(2 * i + n, ring)
            for k in range(CORES):
                source = chip * CORES + k

                @pl.when(source == oj)
                def _():
                    own_slice.wait()

                @pl.when(source != oj)
                def _():
                    gamma_copy(source, source, source).wait_recv()

    def four_terms(i, start=0, size=naux):
        terms = [
            dot_nt(gall[source], block(source, start, size))
            for source in (pick(2 * i + n, ring) * CORES + k for n in range(2) for k in range(CORES))
        ]
        return (terms[0] + terms[1]) + (terms[2] + terms[3])

    def density(i, carry):
        slices_in(i)
        dacc[...] += four_terms(i)
        return carry

    lax.fori_loop(0, 1, density, 0)
    hear(1)
    tell(2)
    lax.fori_loop(1, ROW // CORES // 2 - 1, density, 0)
    hear(2)

    def den_copy(t, row, where, third):
        return pltpu.make_async_remote_copy(
            src_ref=dpart.at[t, third],
            dst_ref=dall.at[row, third],
            send_sem=den_send.at[t, third],
            recv_sem=den_recv.at[row, third],
            device_id=where,
            device_id_type=MESH,
        )

    own_strip = me - first_owner

    def keep_copy():
        return pltpu.make_async_copy(dpart.at[jnp.clip(own_strip, 0, n_oi - 1)], dall.at[oi], local_sem.at[2])

    groups = 4
    final = ROW // CORES // 2 - 1
    wide = naux // 3
    lanes = wide // groups
    slices_in(final)
    for third in range(3):
        columns = slice(third * wide, (third + 1) * wide)
        done = dacc[:, columns] + four_terms(final, third * wide, wide)
        for t in range(n_oi):
            rows = done[t * strip:(t + 1) * strip, :]
            dpart[t, third] = jnp.concatenate(
                [rows[:, g * lanes:(g + 1) * lanes] for g in range(groups)], axis=0
            ).astype(jnp.bfloat16)
        for t in range(n_oi):
            @pl.when(first_owner + t != me)
            def _():
                den_copy(t, oi, owner(t), third).start()

    @pl.when(self_owner)
    def _():
        keep_copy().start()

    for t in range(2):
        out_copy(t).wait()

    def drain(target, carry):
        @pl.when(target != oj)
        def _():
            gamma_copy(target, oj, target).wait_send()
        return carry

    lax.fori_loop(0, ROW, drain, 0)
    @pl.when(self_owner)
    def _():
        keep_copy().wait()

    for row in range(n_oi):
        @pl.when(jnp.logical_or(oi != row, oj != my_slice))
        def _():
            for third in range(3):
                den_copy(0, row, (row, my_slice), third).wait_recv()
    total = dall[0].astype(jnp.float32)
    for row in range(1, n_oi):
        total = total + dall[row].astype(jnp.float32)
    total = total * (1.0 / (n_oi * ROW))
    dens_out[...] = jnp.concatenate(
        [total[third, g * strip:(g + 1) * strip] for third in range(3) for g in range(groups)], axis=1
    ).astype(jnp.bfloat16)

    for t in range(n_oi):
        @pl.when(first_owner + t != me)
        def _():
            for third in range(3):
                den_copy(t, oi, owner(t), third).wait_send()


def body(n_oi, b_tensor, occ_energy, dom_blocks, pair_cols, pao_energy):
    naux, dom = b_tensor.shape[1], b_tensor.shape[2]
    slice_rows = naux // ROW
    strip = slice_rows // n_oi
    vmem = pl.BlockSpec(memory_space=pltpu.VMEM)
    hbm = pl.BlockSpec(memory_space=pl.ANY)
    dma = pltpu.SemaphoreType.DMA
    return pl.pallas_call(
        functools.partial(kernel, n_oi),
        out_shape=(
            jax.ShapeDtypeStruct((1, naux, dom), jnp.bfloat16),
            jax.ShapeDtypeStruct((strip, naux), jnp.bfloat16),
        ),
        in_specs=[hbm, vmem, hbm, hbm, hbm],
        out_specs=(hbm, vmem),
        scratch_shapes=[
            pltpu.SMEM(dom_blocks.shape, jnp.int32),
            pltpu.SMEM(pair_cols.shape, jnp.int32),
            pltpu.VMEM(pao_energy.shape, jnp.float32),
            pltpu.VMEM((ROW, HEAD + naux, dom), jnp.bfloat16),
            pltpu.VMEM((dom, naux), jnp.bfloat16),
            pltpu.VMEM((naux, dom), jnp.float32),
            pltpu.VMEM((naux, dom), jnp.bfloat16),
            pltpu.VMEM((ROW, slice_rows, dom), jnp.bfloat16),
            pltpu.VMEM((dom, CORES * dom), jnp.bfloat16),
            pltpu.VMEM((slice_rows, naux), jnp.float32),
            pltpu.VMEM((n_oi, 3, 4 * strip, naux // 12), jnp.bfloat16),
            pltpu.VMEM((n_oi, 3, 4 * strip, naux // 12), jnp.bfloat16),
            pltpu.VMEM((dom, 128), jnp.float32),
            dma((4, 24)),
            dma((ROW, 3)),
            dma((ROW,)),
            dma((ROW,)),
            dma((n_oi, 3)),
            dma((n_oi, 3)),
            dma((8,)),
            pltpu.SemaphoreType.REGULAR((3,)),
        ],
        compiler_params=pltpu.CompilerParams(
            collective_id=0, has_side_effects=True, vmem_limit_bytes=52 * 2**20
        ),
        cost_estimate=pl.CostEstimate(
            flops=2 * naux * dom * dom * 32, bytes_accessed=4 * naux * dom, transcendentals=0
        ),
    )(b_tensor, occ_energy.reshape(1, 1), dom_blocks, pair_cols, pao_energy)


def solution(mesh):
    in_specs = (
        P(("oi", "oj"), None, None),
        P(("oi", "oj")),
        P(("oi", "oj"), None),
        P(("oi", "oj"), None),
        P(),
    )
    out_specs = (P(("oi", "oj"), None, None), P(("oi", "oj"), None))
    return jax.shard_map(
        functools.partial(body, mesh.shape["oi"]),
        mesh=mesh, in_specs=in_specs, out_specs=out_specs, check_vma=False,
    )
```
